128 devices in a mesh: section: 8 (over y, core), ep: 16 (over z, x).
Axes of the slice: x: 4, y: 4, z: 4, core: 2. Of those that a mesh axis runs over, the one named last changes fastest.
Arguments:
- forward_input: bfloat16 [8, 2048, 2048], P('section', 'ep'), may hold values from -6 to 6
- backward_input: bfloat16 [8, 2048, 2048], P('section', 'ep'), may hold values from -6 to 6
- backward_grad: bfloat16 [8, 2048, 2048], P('section', 'ep'), may hold values from -6 to 6
- forward_routes: int32 [8, 2048, 2], P('section', 'ep'), may hold values from 0 to 31, all different within a row; in each aligned block of 128 rows (0 to 127, 128 to 255, ..., all dimensions but the last counted through in order) at most 24 rows name the same one
- backward_routes: int32 [8, 2048, 2], P('section', 'ep'), may hold values from 0 to 31, all different within a row; in each aligned block of 128 rows (0 to 127, 128 to 255, ..., all dimensions but the last counted through in order) at most 24 rows name the same one
- forward_times: int32 [8, 8], P('section'), may hold values from 0 to 15
- backward_times: int32 [8, 8], P('section'), may hold values from 0 to 15
- modulation: bfloat16 [8, 16, 3, 2048], P('section'), may hold values from -3 to 3
- router_weight: bfloat16 [8, 2048, 32], P('section'), may hold values from -0.125 to 0.125
- expert_up: bfloat16 [8, 32, 2048, 704], P('section', 'ep'), may hold values from -0.125 to 0.125
- expert_down: bfloat16 [8, 32, 704, 2048], P('section', 'ep'), may hold values from -0.21875 to 0.21875
Outputs:
- forward_output: bfloat16 [8, 2048, 2048], P('section', 'ep')
- input_grad: bfloat16 [8, 2048, 2048], P('section', 'ep')
- up_grad: bfloat16 [8, 32, 2048, 704], P('section', 'ep')
- down_grad: bfloat16 [8, 32, 704, 2048], P('section', 'ep')
- router_grad: float32 [8, 2048, 32], P('section')
- modulation_grad: float32 [8, 16, 3, 2048], P('section')
The draws below stay inside these ranges and needn't reach their ends.
Inputs may be any that keep to these rules, and one draw needn't show every extreme that they name: `forward_routes`: in each device's 128 rows no expert is named by more than 24 rows and one expert by exactly 24; a token's two experts differ. `backward_routes`: as for forward_routes.
All inputs are finite; a program needn't handle non-finite values.
Results may differ from the reference program's by a relative error of at most 0.019.
Values may be sent and summed in bfloat16 or wider, within the bound.
A program may use at most 128 MiB of HBM per device.

```python
import math
import jax
import jax.numpy as jnp
import numpy as np
from jax import lax

D = 2048
FF = 704
TOK_DEV = 128
PATCHES = 256
TSTEPS = 16
EXPERTS = 32
TOKENS = 2048
IMAGES = 8
CAP = 24
N_SECTION = 8
N_EP = 16


def place_ends(entries, own_key, least, top_value):
    longest = entries.shape.index(max(entries.shape))
    spots = []
    for shift in (0, 1):
        where = [jax.random.randint(jax.random.fold_in(own_key, axis), (), 0, length) for axis, length in enumerate(entries.shape)]
        where[longest] = (where[longest] + shift) % entries.shape[longest]
        spots.append(tuple(where))
    return entries.at[spots[0]].set(least).at[spots[1]].set(top_value)


def block_scale(rng, dims, pieces, smallest, top_value):
    def one(position, shards_of):
        draws = jax.random.uniform(jax.random.fold_in(jax.random.fold_in(rng, 6), position), (shards_of,), jnp.float32, smallest / len(pieces), top_value / len(pieces))
        return jnp.repeat(jnp.exp(draws), dims[position] // shards_of).reshape((-1,) + (1,) * (len(dims) - position - 1))

    factor_of = one(*pieces[0])
    for cut in pieces[1:]:
        factor_of = factor_of * one(*cut)
    return factor_of


def assign_block(key, own, number, rows, number_of, top, limit, skew):
    ranking = jax.random.permutation(key, number_of)
    crowded, common = portions_of(number_of, rows * top, limit, skew, True), portions_of(number_of, rows * top, limit, skew, False)
    places = jnp.arange(number_of)

    def named(lengths, rotation):
        used = int((lengths > 0).sum())
        fixed = max(1, used // 4)
        passed = fixed + (places - fixed + rotation * (used - fixed)) % max(1, number_of - fixed)
        return jnp.zeros((number_of,), jnp.int32).at[ranking[jnp.where(places < fixed, places, passed)]].set(jnp.asarray(lengths, jnp.int32))

    lengths = jnp.where(number % 4 == 0, named(crowded, number // 4), named(common, number - number // 4 - 1))
    mixed = jax.random.permutation(jax.random.fold_in(own, 3), number_of)
    donor, sink = mixed[0:number_of // 2 * 2:2], mixed[1:number_of // 2 * 2:2]
    margin = jnp.minimum(lengths[donor] - 1, limit - lengths[sink]) // 2
    margin = jnp.where((donor == ranking[0]) | (sink == ranking[0]) | (lengths[sink] == 0), 0, jnp.maximum(margin, 0))
    passed = jax.random.randint(jax.random.fold_in(own, 4), (number_of // 2,), 0, 1 << 20) % (margin + 1)
    lengths = lengths.at[donor].add(-passed).at[sink].add(passed)
    labels = jnp.searchsorted(jnp.cumsum(lengths), jnp.arange(rows * top), side="right").astype(jnp.int32)
    grid = labels.reshape(top, rows).T
    grid = grid[jax.random.permutation(jax.random.fold_in(own, 1), rows)]
    rotation = jax.random.randint(jax.random.fold_in(own, 2), (rows, 1), 0, top)
    return jnp.take_along_axis(grid, (jnp.arange(top)[None, :] + rotation) % top, axis=1)


def portions_of(amount, total, reach, slope, full):
    weights = [(1 << 20) // math.isqrt(grade ** slope) + 1 for grade in range(1, amount + 1)]
    largest = reach if full else min(reach, max(-(-total // amount), total * weights[0] // sum(weights)))
    least = 1 if total - largest >= amount - 1 else 0
    holding, surplus = [largest] + [least] * (amount - 1), total - largest - least * (amount - 1)
    while surplus > 0:
        candidates = [i for i in range(1, amount) if holding[i] < largest] or [i for i in range(1, amount) if holding[i] < reach]
        whole, budget = sum([weights[i] for i in candidates]), surplus
        for i in candidates:
            addition = min(reach - holding[i], max(1, budget * weights[i] // whole), surplus)
            holding[i] = holding[i] + addition
            surplus = surplus - addition
    return np.array(holding)


def bell_draw(key, extent, scale, limit, cuts=(), kind=jnp.bfloat16):
    drawn = jax.random.normal(key, extent, jnp.float32) * scale
    if len(cuts) > 0:
        drawn = block_scale(key, extent, cuts, -0.22, 0.18) * drawn
    return jnp.clip(drawn, min=-limit, max=limit).astype(kind)


def setup_inputs(seed: int = 0) -> dict:
    seeds = jax.random.split(jax.random.key(seed), 12)
    forward_input = bell_draw(seeds[0], (N_SECTION, TOKENS, D), 1.0, 6.0, ((0, 8), (1, 16)))
    backward_input = bell_draw(seeds[1], (N_SECTION, TOKENS, D), 1.0, 6.0, ((0, 8), (1, 16)))
    backward_grad = bell_draw(seeds[2], (N_SECTION, TOKENS, D), 1.0, 6.0, ((0, 8), (1, 16)))
    forward_routes_keys = jax.random.split(jax.random.fold_in(seeds[3], 1), N_SECTION * TOKENS // TOK_DEV)
    forward_routes_turns = jax.random.permutation(jax.random.fold_in(seeds[3], 3), N_SECTION * TOKENS // TOK_DEV)
    forward_routes = jax.vmap(lambda own, number: assign_block(jax.random.fold_in(seeds[3], 2), own, number, TOK_DEV, EXPERTS, 2, CAP, 2))(forward_routes_keys, forward_routes_turns).reshape((N_SECTION, TOKENS, 2))
    backward_routes_keys = jax.random.split(jax.random.fold_in(seeds[4], 1), N_SECTION * TOKENS // TOK_DEV)
    backward_routes_turns = jax.random.permutation(jax.random.fold_in(seeds[4], 3), N_SECTION * TOKENS // TOK_DEV)
    backward_routes = jax.vmap(lambda own, number: assign_block(jax.random.fold_in(seeds[4], 2), own, number, TOK_DEV, EXPERTS, 2, CAP, 2))(backward_routes_keys, backward_routes_turns).reshape((N_SECTION, TOKENS, 2))
    forward_times = place_ends(jax.random.randint(seeds[5], (N_SECTION, IMAGES), 0, TSTEPS), jax.random.fold_in(seeds[5], 1), 0, TSTEPS - 1).astype(jnp.int32)
    backward_times = place_ends(jax.random.randint(seeds[6], (N_SECTION, IMAGES), 0, TSTEPS), jax.random.fold_in(seeds[6], 1), 0, TSTEPS - 1).astype(jnp.int32)
    modulation = bell_draw(seeds[7], (N_SECTION, TSTEPS, 3, D), 0.5, 3.0, ((0, 8),))
    router_weight = bell_draw(seeds[8], (N_SECTION, D, EXPERTS), D ** -0.5, 0.125, ((0, 8),))
    expert_up = bell_draw(seeds[9], (N_SECTION, EXPERTS, D, FF), D ** -0.5, 0.125, ((0, 8), (1, 16)))
    expert_down = bell_draw(seeds[10], (N_SECTION, EXPERTS, FF, D), FF ** -0.5, 0.21875, ((0, 8), (1, 16)))
    return {"forward_input": forward_input, "backward_input": backward_input, "backward_grad": backward_grad, "forward_routes": forward_routes, "backward_routes": backward_routes, "forward_times": forward_times, "backward_times": backward_times, "modulation": modulation, "router_weight": router_weight, "expert_up": expert_up, "expert_down": expert_down}


epsilon = 1e-06
highest = lax.Precision.HIGHEST

def gelu_tanh(values):
    return jax.nn.gelu(values, approximate=True)

def gelu_slope(values):
    return jax.jvp(gelu_tanh, (values,), (jnp.ones_like(values),))[1]

def normalize(inputs):
    values = inputs.astype(jnp.float32)
    center = lax.optimization_barrier(jnp.mean(values, axis=-1, keepdims=True))
    centered = values - center
    variance = lax.optimization_barrier(jnp.mean(centered * centered, axis=-1, keepdims=True))
    inv_std = lax.rsqrt(variance + epsilon)
    return (centered * inv_std, inv_std)

def modulate(token_times, table):
    step_count = table.shape[0]
    onehot = (token_times[:, None] == jnp.arange(step_count, dtype=jnp.int32)[None, :]).astype(jnp.float32)
    flat = table.reshape(step_count, -1).astype(jnp.float32)
    return jnp.dot(onehot, flat, precision=highest).reshape(token_times.shape[0], 3, table.shape[2])

def slot_index(routes, expert_count, capacity):
    flat = routes.reshape(-1)
    onehot = (flat[:, None] == jnp.arange(expert_count, dtype=jnp.int32)[None, :]).astype(jnp.int32)
    ranks = lax.optimization_barrier(jnp.sum((jnp.cumsum(onehot, axis=0) - 1) * onehot, axis=1))
    return (flat * capacity + ranks).reshape(routes.shape).astype(jnp.int32)

def top_gates(mixed_in, router, routes):
    logits = jnp.dot(mixed_in, router, preferred_element_type=jnp.float32)
    picked = jnp.take_along_axis(logits, routes, axis=1)
    first = jax.nn.sigmoid(picked[:, 0] - picked[:, 1])
    second = jax.nn.sigmoid(picked[:, 1] - picked[:, 0])
    return jnp.stack([first, second], axis=1)

def source_backward(grad_in, mix_grad, gathered, slot_back, top_probs, routes, normed, inv_std, modulation_rows, mixed_in, router, token_times, step_count):
    gathered_f = gathered.astype(jnp.float32)
    prob_grad = lax.optimization_barrier(jnp.sum(gathered_f * mix_grad.astype(jnp.float32)[:, None, :], axis=2))
    combined = lax.optimization_barrier(jnp.sum(top_probs[:, :, None] * gathered_f, axis=1))
    logit_step = (prob_grad[:, 0] - prob_grad[:, 1]) * top_probs[:, 0] * top_probs[:, 1]
    expert_ids = jnp.arange(router.shape[1], dtype=jnp.int32)[None, :]
    selector = (routes[:, 0:1] == expert_ids).astype(jnp.float32) - (routes[:, 1:2] == expert_ids).astype(jnp.float32)
    logit_grad = selector * logit_step[:, None]
    router_part = jnp.einsum('td,te->de', mixed_in.astype(jnp.float32), logit_grad, precision=highest)
    mixed_grad = slot_back[:, 0].astype(jnp.float32) + slot_back[:, 1].astype(jnp.float32)
    mixed_grad = mixed_grad + jnp.einsum('te,de->td', logit_grad, router.astype(jnp.float32), precision=highest)
    norm_grad = mixed_grad * (1.0 + modulation_rows[:, 1])
    grad_f = grad_in.astype(jnp.float32)
    input_part = grad_f + inv_std * (norm_grad - lax.optimization_barrier(jnp.mean(norm_grad, axis=-1, keepdims=True)) - normed * lax.optimization_barrier(jnp.mean(norm_grad * normed, axis=-1, keepdims=True)))
    terms = jnp.stack([mixed_grad, mixed_grad * normed, grad_f * combined], axis=1)
    onehot = (token_times[:, None] == jnp.arange(step_count, dtype=jnp.int32)[None, :]).astype(jnp.float32)
    table_part = jnp.dot(onehot.T, terms.reshape(terms.shape[0], -1), precision=highest).reshape(step_count, 3, -1)
    return (input_part.astype(jnp.bfloat16), router_part, table_part)

def prepare(inputs, times_img, routes, table, router):
    count = inputs.shape[0]
    image_ids = jnp.arange(count, dtype=jnp.int32) // PATCHES
    token_times = times_img[image_ids]
    modulation_rows = modulate(token_times, table)
    normed, inv_std = normalize(inputs)
    mixed_in = (normed * (1.0 + modulation_rows[:, 1]) + modulation_rows[:, 0]).astype(jnp.bfloat16)
    top_probs = top_gates(mixed_in, router, routes)
    slot_ids = jax.vmap(lambda block: slot_index(block, EXPERTS, CAP))(routes.reshape(N_EP, TOK_DEV, 2)).reshape(count, 2)
    return (token_times, modulation_rows, normed, inv_std, mixed_in, top_probs, slot_ids)

def source_of():
    return jnp.broadcast_to((jnp.arange(TOKENS, dtype=jnp.int32) // TOK_DEV)[:, None], (TOKENS, 2))

def dispatch(values, slot_ids):
    width = values.shape[-1]
    buffer = jnp.zeros((N_EP, EXPERTS * CAP, width), values.dtype).at[source_of(), slot_ids].set(values)
    return buffer.reshape(N_EP, EXPERTS, CAP, width).transpose(1, 0, 2, 3).reshape(EXPERTS, N_EP * CAP, width)

def collect(buffer, slot_ids):
    width = buffer.shape[-1]
    source_major = buffer.reshape(EXPERTS, N_EP, CAP, width).transpose(1, 0, 2, 3).reshape(N_EP, EXPERTS * CAP, width)
    return source_major[source_of(), slot_ids]

def experts_apply(slot_rows, up_w, down_w):
    pre_gelu = jnp.einsum('erd,edf->erf', slot_rows.astype(jnp.float32), up_w.astype(jnp.float32), precision=highest)
    hidden = gelu_tanh(pre_gelu).astype(jnp.bfloat16)
    expert_out = jnp.einsum('erf,efd->erd', hidden.astype(jnp.float32), down_w.astype(jnp.float32), precision=highest).astype(jnp.bfloat16)
    return (pre_gelu, hidden, expert_out)

def experts_backward(mix_rows, prob_rows, pre_gelu, up_w, down_w):
    out_grad = (prob_rows.astype(jnp.float32) * mix_rows.astype(jnp.float32)).astype(jnp.bfloat16)
    hidden_grad = jnp.einsum('erd,efd->erf', out_grad.astype(jnp.float32), down_w.astype(jnp.float32), precision=highest)
    pre_grad = (hidden_grad * gelu_slope(pre_gelu)).astype(jnp.bfloat16)
    slot_grad = jnp.einsum('erf,edf->erd', pre_grad.astype(jnp.float32), up_w.astype(jnp.float32), precision=highest).astype(jnp.bfloat16)
    return (out_grad, pre_grad, slot_grad)

def reference(forward_input, backward_input, backward_grad, forward_routes, backward_routes, forward_times, backward_times, modulation, router_weight, expert_up, expert_down):
    ahead, behind, up_grads, down_grads, router_grads, table_grads = ([], [], [], [], [], [])
    for section in range(N_SECTION):
        table = modulation[section]
        router = router_weight[section]
        up_w = expert_up[section]
        down_w = expert_down[section]
        token_times, modulation_rows, normed, inv_std, mixed_in, top_probs, slot_ids = prepare(forward_input[section], forward_times[section], forward_routes[section], table, router)
        slot_rows = dispatch(jnp.broadcast_to(mixed_in[:, None, :], (TOKENS, 2, D)), slot_ids)
        pre_gelu, hidden, expert_out = experts_apply(slot_rows, up_w, down_w)
        gathered = collect(expert_out, slot_ids).astype(jnp.float32)
        combined = lax.optimization_barrier(jnp.sum(top_probs[:, :, None] * gathered, axis=1))
        ahead.append((forward_input[section].astype(jnp.float32) + modulation_rows[:, 2] * combined).astype(jnp.bfloat16))
        token_times, modulation_rows, normed, inv_std, mixed_in, top_probs, slot_ids = prepare(backward_input[section], backward_times[section], backward_routes[section], table, router)
        grad_in = backward_grad[section]
        mix_grad = (grad_in.astype(jnp.float32) * modulation_rows[:, 2]).astype(jnp.bfloat16)
        slot_rows = dispatch(jnp.broadcast_to(mixed_in[:, None, :], (TOKENS, 2, D)), slot_ids)
        mix_rows = dispatch(jnp.broadcast_to(mix_grad[:, None, :], (TOKENS, 2, D)), slot_ids)
        prob_rows = dispatch(top_probs.astype(jnp.bfloat16)[:, :, None], slot_ids)
        pre_gelu, hidden, expert_out = experts_apply(slot_rows, up_w, down_w)
        out_grad, pre_grad, slot_grad = experts_backward(mix_rows, prob_rows, pre_gelu, up_w, down_w)
        up_grads.append(jnp.einsum('erd,erf->edf', slot_rows.astype(jnp.float32), pre_grad.astype(jnp.float32), precision=highest).astype(jnp.bfloat16))
        down_grads.append(jnp.einsum('erf,erd->efd', hidden.astype(jnp.float32), out_grad.astype(jnp.float32), precision=highest).astype(jnp.bfloat16))
        gathered = collect(expert_out, slot_ids)
        slot_back = collect(slot_grad, slot_ids)
        input_part, router_part, table_part = source_backward(grad_in, mix_grad, gathered, slot_back, top_probs, backward_routes[section], normed, inv_std, modulation_rows, mixed_in, router, token_times, TSTEPS)
        behind.append(input_part)
        router_grads.append(router_part)
        table_grads.append(table_part)
    forward_output = jnp.roll(jnp.stack(ahead), 1, axis=0)
    input_grad = jnp.roll(jnp.stack(behind), -1, axis=0)
    return (forward_output, input_grad, jnp.stack(up_grads), jnp.stack(down_grads), jnp.stack(router_grads), jnp.stack(table_grads))
```

```python
import jax
import jax.numpy as jnp
from jax import lax
from jax.experimental import pallas as pl
from jax.experimental.pallas import tpu as pltpu
from jax.sharding import PartitionSpec as P

D = 2048
HALF = 1024
FF = 704
TOK = 128
CAP = 24
SLOT = 2 * CAP
EXPERTS = 32
IMAGES = 8
ROWS = IMAGES * SLOT
STAT = 56
TILE = 512
epsilon = 1e-06
MESH = pl.DeviceIdType.MESH
f32 = jnp.float32
bf16 = jnp.bfloat16
FF_TILES = ((0, 256), (256, 512), (512, 704))
PROB, PROB2, OTHER, MU, ISTD, PGRAD = (slice(k, k + 1) for k in range(6))
GELU_A = 0.7978845608028654
GELU_B = 0.044715


def dot(a, b):
    return jnp.dot(a, b, preferred_element_type=f32)


def dot_nt(a, b):
    return lax.dot_general(a, b, (((1,), (1,)), ((), ())), preferred_element_type=f32)


def dot_tn(a, b):
    return lax.dot_general(a, b, (((0,), (0,)), ((), ())), preferred_element_type=f32)


def gelu(values):
    inner = jnp.tanh(GELU_A * (values + GELU_B * values * values * values))
    return 0.5 * values * (1.0 + inner)


def gelu_slope(values):
    square = values * values
    inner = jnp.tanh(GELU_A * (values + GELU_B * values * square))
    outer = 0.5 * values * (1.0 - inner * inner) * (GELU_A * (1.0 + 3.0 * GELU_B * square))
    return 0.5 * (1.0 + inner) + outer


def loop(count, body):
    def step(index, carry):
        body(index)
        return carry

    lax.fori_loop(0, count, step, 0)


class Sems:
    def __init__(self, send, recv, local):
        self.send, self.recv, self.local = send, recv, local
        self.remote_used = self.local_used = 0

    def remote(self, src, dst, device):
        k = self.remote_used
        self.remote_used += 1
        return pltpu.make_async_remote_copy(
            src_ref=src,
            dst_ref=dst,
            send_sem=self.send.at[k],
            recv_sem=self.recv.at[k],
            device_id=device,
            device_id_type=MESH,
        )

    def copy(self, src, dst):
        k = self.local_used
        self.local_used += 1
        return pltpu.make_async_copy(src, dst, self.local.at[k])


N_REMOTE = 110
N_LOCAL = 40


def layer_kernel(
    routes_f,
    routes_b,
    times_f,
    times_b,
    table_ref,
    router_ref,
    xf_hbm,
    xb_hbm,
    dy_hbm,
    up_hbm,
    down_hbm,
    out_f,
    out_b,
    xm_out,
    og_out,
    hid_out,
    pg_out,
    fin_out,
    send_sem,
    recv_sem,
    local_sem,
    meta,
    onehot,
    ag_xb,
    ag_dy,
    ag_xf,
    sb_0,
    sb_1,
    sl_xb,
    sl_dy,
    sl_xf,
    rr_b,
    rr_f,
    hop_b,
    hop_f,
    last_b,
    last_f,
    own,
    up,
    down,
    xm,
    og,
    pre,
    hid,
    pgr,
    tile_out,
    modr,
    cols,
    wrow,
    stat,
    st_z,
    st_2,
    st_x,
    fin,
    res,
):
    section = lax.axis_index("section")
    me = lax.axis_index("ep")
    z, x = me // 4, me % 4
    sems = Sems(send_sem, recv_sem, local_sem)

    def peer(axis, off):
        if axis == 0:
            return (section, lax.rem(z + off + 4, 4) * 4 + x)
        return (section, z * 4 + lax.rem(x + off + 4, 4))

    spot = (z, x)

    def at(axis, off):
        return lax.rem(spot[axis] + off + 4, 4)

    own_copies = []
    for source, ag in ((xb_hbm, ag_xb), (dy_hbm, ag_dy), (xf_hbm, ag_xf)):
        for h in (0, 1):
            cp = sems.copy(source.at[0, :, pl.ds(h * HALF, HALF)], ag.at[h, spot[h]])
            cp.start()
            own_copies.append(cp)
    up_copy = sems.copy(up_hbm.at[0], up)
    down_copy = sems.copy(down_hbm.at[0], down)
    up_copy.start()
    down_copy.start()

    expert_rows = lax.broadcasted_iota(jnp.int32, (EXPERTS, TOK), 0).astype(f32)
    earlier = (
        lax.broadcasted_iota(jnp.int32, (TOK, TOK), 0)
        < lax.broadcasted_iota(jnp.int32, (TOK, TOK), 1)
    ).astype(bf16)
    for way in (0, 1):
        routes = routes_b if way else routes_f
        e0 = routes[0:1, :].astype(f32)
        e1 = routes[1:2, :].astype(f32)
        o0 = (expert_rows == e0).astype(f32)
        o1 = (expert_rows == e1).astype(f32)
        rank = dot((o0 + o1).astype(bf16), earlier)
        s0 = e0 * CAP + jnp.sum(o0 * rank, axis=0, keepdims=True)
        s1 = e1 * CAP + jnp.sum(o1 * rank, axis=0, keepdims=True)
        for k, row in enumerate((s0, s1, e0, e1)):
            meta[x, z, 4 * way + k : 4 * way + k + 1, :] = row

    barrier = pltpu.get_barrier_semaphore()
    for axis in (0, 1):
        for off in (1, 2, 3):
            pl.semaphore_signal(barrier, inc=1, device_id=peer(axis, off), device_id_type=MESH)
    pl.semaphore_wait(barrier, 6)

    meta_z = [sems.remote(meta.at[x, z], meta.at[x, z], peer(0, off)) for off in (1, 2, 3)]
    for cp in meta_z:
        cp.start()

    for cp in own_copies:
        cp.wait()

    def gather_start(ag):
        copies = []
        for off in (1, 3):
            for h in (0, 1):
                block = ag.at[h, spot[h]]
                cp = sems.remote(block, block, peer(h, off))
                cp.start()
                copies.append(cp)
        return copies

    def gather_forward(ag, first):
        copies = []
        for k, off in enumerate((1, 3)):
            for h in (0, 1):
                first[2 * k + h].wait_recv()
                block = ag.at[h, at(h, -off), pl.ds(64 * k, 64)]
                cp = sems.remote(block, block, peer(h, off))
                cp.start()
                copies.append(cp)
        return copies

    g_xb = gather_start(ag_xb)
    g_dy = gather_start(ag_dy)

    for cp in meta_z:
        cp.wait()
    meta_x = [sems.remote(meta.at[x], meta.at[x], peer(1, off)) for off in (1, 2, 3)]
    for cp in meta_x:
        cp.start()

    time_rows = lax.broadcasted_iota(jnp.int32, (2 * IMAGES, 16), 0)
    time_of = jnp.zeros((2 * IMAGES, 16), jnp.int32)
    for i in range(IMAGES):
        time_of = jnp.where(time_rows == i, times_f[0, i], time_of)
        time_of = jnp.where(time_rows == IMAGES + i, times_b[0, i], time_of)
    chosen = (time_of == lax.broadcasted_iota(jnp.int32, (2 * IMAGES, 16), 1)).astype(f32)
    for c in range(3):
        modr[c] = dot(chosen.astype(bf16), table_ref[0, c])

    def modulation_of(way, i, c, span=slice(0, D)):
        return modr[c, pl.ds(i + IMAGES * way, 1), span]

    slot_rows = lax.broadcasted_iota(jnp.int32, (4 * SLOT, TOK), 0)

    def build_onehot(way, h):
        if h == 0:
            ids = slot_rows + z * 192
        else:
            block = (
                (slot_rows >= 48).astype(jnp.int32)
                + (slot_rows >= 96).astype(jnp.int32)
                + (slot_rows >= 144).astype(jnp.int32)
            )
            ids = slot_rows + block * 144 + x * SLOT
        ids = ids.astype(f32)

        def one(s):
            block = meta[x, s] if h == 0 else meta[s, z]
            s0 = block[4 * way : 4 * way + 1, :]
            s1 = block[4 * way + 1 : 4 * way + 2, :]
            onehot[way, h, s] = ((ids == s0).astype(f32) + (ids == s1).astype(f32)).astype(bf16)

        loop(4, one)

    build_onehot(1, 0)
    for cp in meta_x:
        cp.wait()
    build_onehot(1, 1)
    build_onehot(0, 0)
    build_onehot(0, 1)

    def pack(way, ag, sb, h):
        def one(s):
            for n in (0, 1):
                part = dot(onehot[way, h, s], ag[h, s, :, n * TILE : (n + 1) * TILE])
                sb[h, :, s, :, n * TILE : (n + 1) * TILE] = part.astype(bf16).reshape(4, SLOT, TILE)

        loop(4, one)

    def exchange(sb, rb):
        copies = []
        for off in (2, 1, 3):
            for h in (0, 1):
                axis = 1 - h
                cp = sems.remote(
                    sb.at[h, at(axis, off)], rb.at[h, spot[axis]], peer(axis, off)
                )
                cp.start()
                copies.append(cp)
        local = []
        for h in (0, 1):
            axis = 1 - h
            cp = sems.copy(sb.at[h, spot[axis]], rb.at[h, spot[axis]])
            cp.start()
            local.append(cp)
        return copies, local

    def arrived(copies):
        for cp in copies[0]:
            cp.wait_recv()
        for cp in copies[1]:
            cp.wait()

    def dispatch_pack(way, ag, first, second, sb, rb):
        for cp in second:
            cp.wait_recv()
        for h in (0, 1):
            pack(way, ag, sb, h)
        return exchange(sb, rb)

    f_xb = gather_forward(ag_xb, g_xb)
    g_xf = gather_start(ag_xf)
    a_xb = dispatch_pack(1, ag_xb, g_xb, f_xb, sb_0, sl_xb)
    f_dy = gather_forward(ag_dy, g_dy)
    a_dy = dispatch_pack(1, ag_dy, g_dy, f_dy, sb_1, sl_dy)
    f_xf = gather_forward(ag_xf, g_xf)
    for cp in a_xb[0]:
        cp.wait_send()
    for cp in a_xb[1]:
        cp.wait()
    a_xf = dispatch_pack(0, ag_xf, g_xf, f_xf, sb_0, sl_xf)
    for cp in g_xb + f_xb + g_dy + f_dy + g_xf + f_xf:
        cp.wait_send()

    def slots_of(sl, h, zi, xi):
        block = sl[h, xi, zi] if h == 0 else sl[h, zi, xi]
        return block.astype(f32)

    def by_expert(sl, h, i, j):
        zi, xi = i // 2, 2 * (i % 2)
        first = slots_of(sl, h, zi, xi)[j * CAP : (j + 1) * CAP]
        second = slots_of(sl, h, zi, xi + 1)[j * CAP : (j + 1) * CAP]
        return jnp.concatenate([first, second], axis=0)

    cap_rows = lax.broadcasted_iota(jnp.int32, (CAP, TOK), 0)

    def normalize(sl, way):
        def one(i):
            zi, xi = i // 2, 2 * (i % 2)
            shift, scale = modulation_of(way, i, 0), modulation_of(way, i, 1)
            for j in (0, 1):
                left, right = by_expert(sl, 0, i, j), by_expert(sl, 1, i, j)
                total = jnp.sum(left, axis=1, keepdims=True) + jnp.sum(right, axis=1, keepdims=True)
                center = total * (1.0 / D)
                left, right = left - center, right - center
                total = jnp.sum(left * left, axis=1, keepdims=True) + jnp.sum(
                    right * right, axis=1, keepdims=True
                )
                inv = lax.rsqrt(total * (1.0 / D) + epsilon)
                for h, part in ((0, left), (1, right)):
                    span = slice(h * HALF, (h + 1) * HALF)
                    mixed = part * inv * (1.0 + scale[:, span]) + shift[:, span]
                    xm[j, i, :, span] = mixed.astype(bf16)
                cols[j, i, :, MU] = center
                cols[j, i, :, ISTD] = inv
                ids = (cap_rows + (me * SLOT + j * CAP)).astype(f32)
                found = []
                for par in (0, 1):
                    block = meta[xi + par, zi]
                    s0, s1, e0, e1 = [
                        block[4 * way + k : 4 * way + k + 1, :] for k in range(4)
                    ]
                    hit = jnp.where(ids == s0, e1, 0.0) + jnp.where(ids == s1, e0, 0.0)
                    found.append(jnp.sum(hit, axis=1, keepdims=True))
                cols[j, i, :, OTHER] = jnp.concatenate(found, axis=0)

        loop(IMAGES, one)

    lane = lax.broadcasted_iota(jnp.int32, (ROWS, EXPERTS), 1)

    def picks(j):
        own = (lane == 2 * me + j).astype(f32)
        return own - (lane.astype(f32) == cols[j, :, :, OTHER].reshape(ROWS, 1)).astype(f32)

    def experts_up(keep):
        def one(j):
            rows = xm[j].reshape(ROWS, D)
            logits = dot_nt(rows, router_ref[0])
            gap = jnp.sum(logits * picks(j), axis=1, keepdims=True)
            chance = 1.0 / (1.0 + jnp.exp(-gap))
            cols[j, :, :, PROB] = chance.reshape(IMAGES, SLOT, 1)
            if keep:
                cols[j, :, :, PROB2] = (chance * (1.0 / (1.0 + jnp.exp(gap)))).reshape(IMAGES, SLOT, 1)
            for f0, f1 in FF_TILES:
                part = dot_nt(rows, up[j, f0:f1, :])
                if keep:
                    pre[j, :, f0:f1] = part
                hid[j, :, f0:f1] = gelu(part).astype(bf16)

        loop(2, one)

    def put_rows(sb, h, n):
        def one(i):
            zi, xi = i // 2, 2 * (i % 2)
            a, b = tile_out[0, i], tile_out[1, i]
            for par in (0, 1):
                block = jnp.concatenate(
                    [a[par * CAP : (par + 1) * CAP], b[par * CAP : (par + 1) * CAP]], axis=0
                ).astype(bf16)
                span = slice(n * TILE, (n + 1) * TILE)
                if h == 0:
                    sb[h, xi + par, zi, :, span] = block
                else:
                    sb[h, zi, xi + par, :, span] = block

        loop(IMAGES, one)

    for cp in a_xb[0]:
        cp.wait_recv()
    normalize(sl_xb, 1)
    up_copy.wait()
    experts_up(True)
    down_copy.wait()
    arrived(a_dy)

    stat[...] = jnp.zeros_like(stat)
    cols[:, :, :, PGRAD] = jnp.zeros((2, IMAGES, SLOT, 1), f32)

    def order_dy(i):
        for j in (0, 1):
            for h in (0, 1):
                og[j, i, :, h * HALF : (h + 1) * HALF] = by_expert(sl_dy, h, i, j).astype(bf16)

    loop(IMAGES, order_dy)

    for n in range(D // TILE):
        span = slice(n * TILE, (n + 1) * TILE)

        def out_tile(j):
            part = dot(hid[j], down[j, :, span]).astype(bf16).astype(f32)
            tile_out[j] = part.reshape(IMAGES, SLOT, TILE)

        loop(2, out_tile)

        def out_image(i):
            gate = modulation_of(1, i, 2, span)
            total = jnp.zeros((1, TILE), f32)
            for j in (0, 1):
                out = tile_out[j, i]
                dyv = og[j, i, :, span].astype(f32)
                chance = cols[j, i, :, PROB]
                mix = (dyv * gate).astype(bf16).astype(f32)
                cols[j, i, :, PGRAD] += jnp.sum(out * mix, axis=1, keepdims=True)
                total += jnp.sum(out * dyv * chance, axis=0, keepdims=True)
                og[j, i, :, span] = (chance.astype(bf16).astype(f32) * mix).astype(bf16)
            stat[2, pl.ds(i, 1), span] = total

        loop(IMAGES, out_image)

    def hidden_grad(j):
        rows = og[j].reshape(ROWS, D)
        for f0, f1 in FF_TILES:
            part = dot_nt(rows, down[j, f0:f1, :])
            pgr[j, :, f0:f1] = (part * gelu_slope(pre[j, :, f0:f1])).astype(bf16)
        weight = picks(j) * (cols[j, :, :, PGRAD] * cols[j, :, :, PROB2]).reshape(ROWS, 1)
        high = weight.astype(bf16)
        wrow[j, 0] = high
        wrow[j, 1] = (weight - high.astype(f32)).astype(bf16)

    loop(2, hidden_grad)
    for cp in a_dy[0]:
        cp.wait_send()

    for n in range(D // TILE):
        h = n // 2
        span = slice(n * TILE, (n + 1) * TILE)

        def grad_tile(j):
            part = dot(pgr[j], up[j, :, span]).astype(bf16).astype(f32)
            rows = router_ref[0, :, span]
            part += dot(wrow[j, 0], rows) + dot(wrow[j, 1], rows)
            tile_out[j] = part.reshape(IMAGES, SLOT, TILE)
            block = xm[j].reshape(ROWS, D)[:, span]
            rg = dot_tn(wrow[j, 0], block) + dot_tn(wrow[j, 1], block)
            for k in range(EXPERTS // 8):
                stat[3 + k, :, span] += rg[8 * k : 8 * k + 8]

        loop(2, grad_tile)
        inner = slice((n % 2) * TILE, (n % 2 + 1) * TILE)

        def grad_image(i):
            zi, xi = i // 2, 2 * (i % 2)
            shift = jnp.zeros((1, TILE), f32)
            scale = jnp.zeros((1, TILE), f32)
            for par in (0, 1):
                block = sl_xb[h, xi + par, zi, :, inner] if h == 0 else sl_xb[h, zi, xi + par, :, inner]
                block = block.astype(f32)
                for j in (0, 1):
                    cut = slice(par * CAP, (par + 1) * CAP)
                    grad = tile_out[j, i][cut]
                    normed = (block[j * CAP : (j + 1) * CAP] - cols[j, i, cut, MU]) * cols[j, i, cut, ISTD]
                    shift += jnp.sum(grad, axis=0, keepdims=True)
                    scale += jnp.sum(grad * normed, axis=0, keepdims=True)
            stat[0, pl.ds(i, 1), span] = shift
            stat[1, pl.ds(i, 1), span] = scale

        loop(IMAGES, grad_image)
        put_rows(sb_1, h, n % 2)

    r_b = exchange(sb_1, rr_b)
    kept = []
    for source, dest in ((xm, xm_out), (og, og_out), (hid, hid_out), (pgr, pg_out)):
        cp = sems.copy(source, dest)
        cp.start()
        kept.append(cp)
    sum_z = [
        sems.remote(
            stat.at[:, :, pl.ds(pl.multiple_of(at(0, off) * TILE, TILE), TILE)],
            st_z.at[z],
            peer(0, off),
        )
        for off in (1, 2, 3)
    ]
    for cp in sum_z:
        cp.start()

    arrived(a_xf)
    for cp in kept:
        cp.wait()
    normalize(sl_xf, 0)
    experts_up(False)
    for cp in a_xf[0]:
        cp.wait_send()
    for n in range(D // TILE):
        span = slice(n * TILE, (n + 1) * TILE)

        def give_tile(j):
            part = dot(hid[j], down[j, :, span]) * cols[j, :, :, PROB].reshape(ROWS, 1)
            tile_out[j] = part.reshape(IMAGES, SLOT, TILE)

        loop(2, give_tile)
        put_rows(sb_0, n // 2, n % 2)
    r_f = exchange(sb_0, rr_f)

    for cp in sum_z:
        cp.wait()
    st_z[z] = stat[:, :, pl.ds(pl.multiple_of(z * TILE, TILE), TILE)]
    st_2[...] = st_z[0] + st_z[1] + st_z[2] + st_z[3]
    sum_x = [
        sems.remote(
            st_2.at[:, :, pl.ds(pl.multiple_of(at(1, off) * TOK, TOK), TOK)],
            st_x.at[x],
            peer(1, off),
        )
        for off in (1, 2, 3)
    ]
    for cp in sum_x:
        cp.start()

    def unpack(way, rr, ag, own, hop, h):
        def summed(s):
            block = rr[h, :, s]
            return dot_tn(onehot[way, h, s], block.reshape(4 * SLOT, HALF))

        s = at(h, 2)
        ag[h, s] = summed(s).astype(bf16)
        copies = []
        for k, off in enumerate((1, 3)):
            cp = sems.remote(ag.at[h, s, pl.ds(64 * k, 64)], hop.at[h, k], peer(h, off))
            cp.start()
            copies.append(cp)
        for off in (1, 3):
            s = at(h, off)
            ag[h, s] = summed(s).astype(bf16)
        own[h] = summed(spot[h])
        return copies

    def pass_on(ag, hop, last, first, h):
        copies = []
        for k, off in enumerate((1, 3)):
            first[k].wait_recv()
            s = at(h, off)
            rows = pl.ds(64 * k, 64)
            ag[h, s, rows] = (ag[h, s, rows].astype(f32) + hop[h, k].astype(f32)).astype(bf16)
            cp = sems.remote(ag.at[h, s], last.at[h, k], peer(h, off))
            cp.start()
            copies.append(cp)
        return copies

    def total_of(own, last, second, h):
        for cp in second:
            cp.wait_recv()
        own[h] += last[h, 0].astype(f32) + last[h, 1].astype(f32)

    arrived(r_b)
    hop_copies_b = [unpack(1, rr_b, ag_xb, own, hop_b, h) for h in (0, 1)]
    last_copies_b = [pass_on(ag_xb, hop_b, last_b, hop_copies_b[h], h) for h in (0, 1)]

    for cp in sum_x:
        cp.wait()
    st_x[x] = st_2[:, :, pl.ds(pl.multiple_of(x * TOK, TOK), TOK)]
    own_part = fin.at[:, :, pl.ds(pl.multiple_of(me * TOK, TOK), TOK)]
    own_part[...] = st_x[0] + st_x[1] + st_x[2] + st_x[3]
    give_x = [sems.remote(own_part, own_part, peer(1, off)) for off in (1, 2, 3)]
    for cp in give_x:
        cp.start()

    for h in (0, 1):
        total_of(own, last_b, last_copies_b[h], h)
    own_scale = modulation_of(1, me // 2, 1)

    def input_grads(c):
        at_rows = pl.ds(pl.multiple_of(c * 32, 32), 32)
        parts = []
        for h in (0, 1):
            parts.append(ag_xb[h, spot[h], at_rows].astype(f32))
        total = jnp.sum(parts[0], axis=1, keepdims=True) + jnp.sum(parts[1], axis=1, keepdims=True)
        center = total * (1.0 / D)
        parts = [part - center for part in parts]
        total = jnp.sum(parts[0] * parts[0], axis=1, keepdims=True) + jnp.sum(
            parts[1] * parts[1], axis=1, keepdims=True
        )
        inv = lax.rsqrt(total * (1.0 / D) + epsilon)
        normed = [part * inv for part in parts]
        grads = []
        for h in (0, 1):
            span = slice(h * HALF, (h + 1) * HALF)
            grads.append(own[h, at_rows] * (1.0 + own_scale[:, span]))
        mean = (
            jnp.sum(grads[0], axis=1, keepdims=True) + jnp.sum(grads[1], axis=1, keepdims=True)
        ) * (1.0 / D)
        slope = (
            jnp.sum(grads[0] * normed[0], axis=1, keepdims=True)
            + jnp.sum(grads[1] * normed[1], axis=1, keepdims=True)
        ) * (1.0 / D)
        for h in (0, 1):
            span = slice(h * HALF, (h + 1) * HALF)
            dyv = ag_dy[h, spot[h], at_rows].astype(f32)
            part = dyv + inv * (grads[h] - mean - normed[h] * slope)
            res[at_rows, span] = part.astype(bf16)

    loop(4, input_grads)
    back_copy = sems.copy(res, out_b)
    back_copy.start()

    for cp in give_x:
        cp.wait()
    own_part = fin.at[:, :, pl.ds(pl.multiple_of(z * TILE, TILE), TILE)]
    give_z = [sems.remote(own_part, own_part, peer(0, off)) for off in (1, 2, 3)]
    for cp in give_z:
        cp.start()

    arrived(r_f)
    hop_copies_f = [unpack(0, rr_f, ag_xf, own, hop_f, h) for h in (0, 1)]
    last_copies_f = [pass_on(ag_xf, hop_f, last_f, hop_copies_f[h], h) for h in (0, 1)]
    for h in (0, 1):
        total_of(own, last_f, last_copies_f[h], h)
    back_copy.wait()
    own_gate = modulation_of(0, me // 2, 2)

    def outputs(c):
        at_rows = pl.ds(pl.multiple_of(c * 32, 32), 32)
        for h in (0, 1):
            span = slice(h * HALF, (h + 1) * HALF)
            part = ag_xf[h, spot[h], at_rows].astype(f32) + own_gate[:, span] * own[h, at_rows]
            res[at_rows, span] = part.astype(bf16)

    loop(4, outputs)
    front_copy = sems.copy(res, out_f)
    front_copy.start()
    for cp in give_z:
        cp.wait()
    fin_copy = sems.copy(fin, fin_out)
    fin_copy.start()
    for cp in r_b[0] + r_f[0]:
        cp.wait_send()
    for pair in hop_copies_b + last_copies_b + hop_copies_f + last_copies_f:
        for cp in pair:
            cp.wait_send()
    front_copy.wait()
    fin_copy.wait()


def layer(routes_f, routes_b, times_f, times_b, table, router, xf, xb, dy, up, down):
    any_spec = pl.BlockSpec(memory_space=pl.ANY)
    vmem = pl.BlockSpec(memory_space=pltpu.VMEM)
    smem = pl.BlockSpec(memory_space=pltpu.SMEM)
    shape = jax.ShapeDtypeStruct
    gather = pltpu.VMEM((2, 4, TOK, HALF), bf16)
    slots = pltpu.VMEM((2, 4, 4, SLOT, HALF), bf16)
    return pl.pallas_call(
        layer_kernel,
        out_shape=(
            shape((TOK, D), bf16),
            shape((TOK, D), bf16),
            shape((2, IMAGES, SLOT, D), bf16),
            shape((2, IMAGES, SLOT, D), bf16),
            shape((2, ROWS, FF), bf16),
            shape((2, ROWS, FF), bf16),
            shape((7, 8, D), f32),
        ),
        in_specs=[vmem, vmem, smem, smem, vmem, vmem] + [any_spec] * 5,
        out_specs=tuple([any_spec] * 7),
        scratch_shapes=[
            pltpu.SemaphoreType.DMA((N_REMOTE,)),
            pltpu.SemaphoreType.DMA((N_REMOTE,)),
            pltpu.SemaphoreType.DMA((N_LOCAL,)),
            pltpu.VMEM((4, 4, 8, TOK), f32),
            pltpu.VMEM((2, 2, 4, 4 * SLOT, TOK), bf16),
            gather,
            gather,
            gather,
            slots,
            slots,
            slots,
            slots,
            slots,
            slots,
            slots,
            pltpu.VMEM((2, 2, 64, HALF), bf16),
            pltpu.VMEM((2, 2, 64, HALF), bf16),
            pltpu.VMEM((2, 2, TOK, HALF), bf16),
            pltpu.VMEM((2, 2, TOK, HALF), bf16),
            pltpu.VMEM((2, TOK, HALF), f32),
            pltpu.VMEM((2, FF, D), bf16),
            pltpu.VMEM((2, FF, D), bf16),
            pltpu.VMEM((2, IMAGES, SLOT, D), bf16),
            pltpu.VMEM((2, IMAGES, SLOT, D), bf16),
            pltpu.VMEM((2, ROWS, FF), f32),
            pltpu.VMEM((2, ROWS, FF), bf16),
            pltpu.VMEM((2, ROWS, FF), bf16),
            pltpu.VMEM((2, IMAGES, SLOT, TILE), f32),
            pltpu.VMEM((3, 2 * IMAGES, D), f32),
            pltpu.VMEM((2, IMAGES, SLOT, 8), f32),
            pltpu.VMEM((2, 2, ROWS, EXPERTS), bf16),
            pltpu.VMEM((7, 8, D), f32),
            pltpu.VMEM((4, 7, 8, TILE), f32),
            pltpu.VMEM((7, 8, TILE), f32),
            pltpu.VMEM((4, 7, 8, TOK), f32),
            pltpu.VMEM((7, 8, D), f32),
            pltpu.VMEM((TOK, D), bf16),
        ],
        compiler_params=pltpu.CompilerParams(
            collective_id=0, has_side_effects=True, vmem_limit_bytes=63 << 20
        ),
        cost_estimate=pl.CostEstimate(
            flops=13_000_000_000, bytes_accessed=30_000_000, transcendentals=2_000_000
        ),
        name="moe_layer",
    )(routes_f, routes_b, times_f, times_b, table, router, xf, xb, dy, up, down)


def gradients_kernel(times, pg, hid, xm, og, sums, up_out, down_out, router_out, table_out, pg_t, hid_t):
    n = pl.program_id(1)

    @pl.when(n == 0)
    def _():
        pg_t[...] = pg[0].T
        hid_t[...] = hid[0].T

    up_out[0, 0] = dot(pg_t[...], xm[0]).astype(bf16)
    down_out[0, 0] = dot(hid_t[...], og[0]).astype(bf16)

    @pl.when((n == 0) & (pl.program_id(0) == 0))
    def _():
        for k in range(EXPERTS // 8):
            router_out[0, 8 * k : 8 * k + 8] = sums[3 + k]
        steps = lax.broadcasted_iota(jnp.int32, (16, 1), 0)
        for c in range(3):
            total = jnp.zeros((16, D), f32)
            for i in range(IMAGES):
                total += jnp.where(steps == times[0, i], sums[c, i : i + 1, :], 0.0)
            table_out[0, c] = total


def gradients(times, pg, hid, xm, og, sums):
    shape = jax.ShapeDtypeStruct
    whole = lambda j, n: (j, 0, 0)
    part = lambda j, n: (j, 0, n)
    return pl.pallas_call(
        gradients_kernel,
        grid=(2, D // TILE),
        out_shape=(
            shape((1, 2, FF, D), bf16),
            shape((1, 2, FF, D), bf16),
            shape((1, EXPERTS, D), f32),
            shape((1, 3, 16, D), f32),
        ),
        in_specs=[
            pl.BlockSpec(memory_space=pltpu.SMEM),
            pl.BlockSpec((1, ROWS, FF), whole),
            pl.BlockSpec((1, ROWS, FF), whole),
            pl.BlockSpec((1, ROWS, TILE), part),
            pl.BlockSpec((1, ROWS, TILE), part),
            pl.BlockSpec((7, 8, D), lambda j, n: (0, 0, 0)),
        ],
        out_specs=(
            pl.BlockSpec((1, 1, FF, TILE), lambda j, n: (0, j, 0, n)),
            pl.BlockSpec((1, 1, FF, TILE), lambda j, n: (0, j, 0, n)),
            pl.BlockSpec((1, EXPERTS, D), lambda j, n: (0, 0, 0)),
            pl.BlockSpec((1, 3, 16, D), lambda j, n: (0, 0, 0, 0)),
        ),
        scratch_shapes=[pltpu.VMEM((FF, ROWS), bf16), pltpu.VMEM((FF, ROWS), bf16)],
        compiler_params=pltpu.CompilerParams(vmem_limit_bytes=40 << 20),
        cost_estimate=pl.CostEstimate(
            flops=4_500_000_000, bytes_accessed=22_000_000, transcendentals=0
        ),
        name="weight_grads",
    )(times, pg, hid, xm, og, sums)


def passed_along(value, steps):
    count = lax.axis_size("section")
    pairs = [(source, (source + steps) % count) for source in range(count)]
    return lax.ppermute(value, "section", pairs)


def per_device(
    forward_input,
    backward_input,
    backward_grad,
    forward_routes,
    backward_routes,
    forward_times,
    backward_times,
    modulation,
    router_weight,
    expert_up,
    expert_down,
):
    block_out, input_part, rows, out_grad, hidden, pre_grad, sums = layer(
        forward_routes[0].T,
        backward_routes[0].T,
        forward_times,
        backward_times,
        modulation.transpose(0, 2, 1, 3),
        router_weight.transpose(0, 2, 1),
        forward_input,
        backward_input,
        backward_grad,
        expert_up.transpose(0, 1, 3, 2),
        expert_down,
    )
    input_grad = passed_along(input_part, -1)
    forward_output = passed_along(block_out, 1)
    rows = rows.reshape(2, ROWS, D)
    out_grad = out_grad.reshape(2, ROWS, D)
    up_grad, down_grad, router_grad, table_grad = gradients(
        backward_times, pre_grad, hidden, rows, out_grad, sums
    )
    return (
        forward_output[None],
        input_grad[None],
        up_grad.transpose(0, 1, 3, 2),
        down_grad,
        router_grad.transpose(0, 2, 1),
        table_grad.transpose(0, 2, 1, 3),
    )


def solution(mesh):
    placed = (
        P("section", "ep", None),
        P("section", "ep", None),
        P("section", "ep", None),
        P("section", "ep", None),
        P("section", "ep", None),
        P("section", None),
        P("section", None),
        P("section", None, None, None),
        P("section", None, None),
        P("section", "ep", None, None),
        P("section", "ep", None, None),
    )
    return jax.shard_map(
        per_device,
        mesh=mesh,
        in_specs=placed,
        out_specs=(
            P("section", "ep", None),
            P("section", "ep", None),
            P("section", "ep", None, None),
            P("section", "ep", None, None),
            P("section", None, None),
            P("section", None, None, None),
        ),
        check_vma=False,
    )
```

```python
import jax
import jax.numpy as jnp
from jax import lax
from jax.experimental import pallas as pl
from jax.experimental.pallas import tpu as pltpu
from jax.sharding import PartitionSpec as P

D = 2048
HALF = 1024
FF = 704
TOK = 128
CAP = 24
SLOT = 2 * CAP
EXPERTS = 32
IMAGES = 8
ROWS = IMAGES * SLOT
STAT = 56
TILE = 512
epsilon = 1e-06
MESH = pl.DeviceIdType.MESH
f32 = jnp.float32
bf16 = jnp.bfloat16
FF_TILES = ((0, 256), (256, 512), (512, 704))
PROB, PROB2, OTHER, PGRAD, MU_B, ISTD_B = (slice(k, k + 1) for k in range(6))
GELU_A = 0.7978845608028654
GELU_B = 0.044715


def dot(a, b):
    return jnp.dot(a, b, preferred_element_type=f32)


def dot_nt(a, b):
    return lax.dot_general(a, b, (((1,), (1,)), ((), ())), preferred_element_type=f32)


def dot_tn(a, b):
    return lax.dot_general(a, b, (((0,), (0,)), ((), ())), preferred_element_type=f32)


def gelu(values):
    inner = jnp.tanh(GELU_A * (values + GELU_B * values * values * values))
    return 0.5 * values * (1.0 + inner)


def gelu_slope(values):
    square = values * values
    inner = jnp.tanh(GELU_A * (values + GELU_B * values * square))
    outer = 0.5 * values * (1.0 - inner * inner) * (GELU_A * (1.0 + 3.0 * GELU_B * square))
    return 0.5 * (1.0 + inner) + outer


def loop(count, body):
    def step(index, carry):
        body(index)
        return carry

    lax.fori_loop(0, count, step, 0)


class Sems:
    def __init__(self, send, recv, local):
        self.send, self.recv, self.local = send, recv, local
        self.remote_used = self.local_used = 0

    def remote(self, src, dst, device):
        k = self.remote_used
        self.remote_used += 1
        return pltpu.make_async_remote_copy(
            src_ref=src,
            dst_ref=dst,
            send_sem=self.send.at[k],
            recv_sem=self.recv.at[k],
            device_id=device,
            device_id_type=MESH,
        )

    def copy(self, src, dst):
        k = self.local_used
        self.local_used += 1
        return pltpu.make_async_copy(src, dst, self.local.at[k])


N_REMOTE = 200
N_LOCAL = 40


def layer_kernel(
    routes_f,
    routes_b,
    times_f,
    times_b,
    table_ref,
    router_ref,
    xf_hbm,
    xb_hbm,
    dy_hbm,
    up_hbm,
    down_hbm,
    out_f,
    out_b,
    xm_out,
    og_out,
    hid_out,
    pg_out,
    fin_out,
    send_sem,
    recv_sem,
    local_sem,
    meta,
    onehot,
    ag_xb,
    ag_dy,
    ag_xf,
    sb_0,
    sb_1,
    sl_xb,
    sl_dy,
    sl_xf,
    rr_b,
    rr_f,
    hop_b,
    hop_f,
    last_b,
    last_f,
    own,
    up,
    down,
    xm,
    og,
    pre,
    hid,
    pgr,
    tile_out,
    modr,
    cols,
    wrow,
    stat,
    st_z,
    st_2,
    st_x,
    fin,
    res,
):
    section = lax.axis_index("section")
    me = lax.axis_index("ep")
    z, x = me // 4, me % 4
    sems = Sems(send_sem, recv_sem, local_sem)

    def peer(axis, off):
        if axis == 0:
            return (section, lax.rem(z + off + 4, 4) * 4 + x)
        return (section, z * 4 + lax.rem(x + off + 4, 4))

    spot = (z, x)

    def at(axis, off):
        return lax.rem(spot[axis] + off + 4, 4)

    own_copies = []
    for source, ag in ((xb_hbm, ag_xb), (dy_hbm, ag_dy), (xf_hbm, ag_xf)):
        for h in (0, 1):
            cp = sems.copy(source.at[0, :, pl.ds(h * HALF, HALF)], ag.at[h, spot[h]])
            cp.start()
            own_copies.append(cp)
    up_copy = sems.copy(up_hbm.at[0], up)
    down_copy = sems.copy(down_hbm.at[0], down)
    up_copy.start()
    down_copy.start()

    expert_rows = lax.broadcasted_iota(jnp.int32, (EXPERTS, TOK), 0).astype(f32)
    earlier = (
        lax.broadcasted_iota(jnp.int32, (TOK, TOK), 0)
        < lax.broadcasted_iota(jnp.int32, (TOK, TOK), 1)
    ).astype(bf16)
    for way in (0, 1):
        routes = routes_b if way else routes_f
        e0 = routes[0:1, :].astype(f32)
        e1 = routes[1:2, :].astype(f32)
        o0 = (expert_rows == e0).astype(f32)
        o1 = (expert_rows == e1).astype(f32)
        rank = dot((o0 + o1).astype(bf16), earlier)
        s0 = e0 * CAP + jnp.sum(o0 * rank, axis=0, keepdims=True)
        s1 = e1 * CAP + jnp.sum(o1 * rank, axis=0, keepdims=True)
        for k, row in enumerate((s0, s1, e0, e1)):
            meta[x, z, 4 * way + k : 4 * way + k + 1, :] = row

    barrier = pltpu.get_barrier_semaphore()
    for axis in (0, 1):
        for off in (1, 2, 3):
            pl.semaphore_signal(barrier, inc=1, device_id=peer(axis, off), device_id_type=MESH)
    pl.semaphore_wait(barrier, 6)

    meta_z = [sems.remote(meta.at[x, z], meta.at[x, z], peer(0, off)) for off in (1, 2, 3)]
    for cp in meta_z:
        cp.start()

    for cp in own_copies:
        cp.wait()

    def gather_start(ag):
        copies = []
        for off in (1, 3):
            for h in (0, 1):
                block = ag.at[h, spot[h]]
                cp = sems.remote(block, block, peer(h, off))
                cp.start()
                copies.append(cp)
        return copies

    def gather_forward(ag, first):
        copies = []
        for k, off in enumerate((1, 3)):
            for h in (0, 1):
                first[2 * k + h].wait_recv()
                block = ag.at[h, at(h, -off), pl.ds(64 * k, 64)]
                cp = sems.remote(block, block, peer(h, off))
                cp.start()
                copies.append(cp)
        return copies

    g_xb = gather_start(ag_xb)
    g_dy = gather_start(ag_dy)

    for cp in meta_z:
        cp.wait()
    meta_x = [sems.remote(meta.at[x], meta.at[x], peer(1, off)) for off in (1, 2, 3)]
    for cp in meta_x:
        cp.start()

    time_rows = lax.broadcasted_iota(jnp.int32, (2 * IMAGES, 16), 0)
    time_of = jnp.zeros((2 * IMAGES, 16), jnp.int32)
    for i in range(IMAGES):
        time_of = jnp.where(time_rows == i, times_f[0, i], time_of)
        time_of = jnp.where(time_rows == IMAGES + i, times_b[0, i], time_of)
    chosen = (time_of == lax.broadcasted_iota(jnp.int32, (2 * IMAGES, 16), 1)).astype(f32)
    for c in range(3):
        modr[c] = dot(chosen.astype(bf16), table_ref[0, c])

    def modulation_of(way, i, c, span=slice(0, D)):
        return modr[c, pl.ds(i + IMAGES * way, 1), span]

    slot_rows = lax.broadcasted_iota(jnp.int32, (4 * SLOT, TOK), 0)

    def build_onehot(way, h):
        if h == 0:
            ids = slot_rows + z * 192
        else:
            block = (
                (slot_rows >= 48).astype(jnp.int32)
                + (slot_rows >= 96).astype(jnp.int32)
                + (slot_rows >= 144).astype(jnp.int32)
            )
            ids = slot_rows + block * 144 + x * SLOT
        ids = ids.astype(f32)

        def one(s):
            block = meta[x, s] if h == 0 else meta[s, z]
            s0 = block[4 * way : 4 * way + 1, :]
            s1 = block[4 * way + 1 : 4 * way + 2, :]
            onehot[way, h, s] = ((ids == s0).astype(f32) + (ids == s1).astype(f32)).astype(bf16)

        loop(4, one)

    def pack(way, ag, sb, h, s):
        for n in (0, 1):
            part = dot(onehot[way, h, s], ag[h, s, :, n * TILE : (n + 1) * TILE])
            sb[h, :, s, :, n * TILE : (n + 1) * TILE] = part.astype(bf16).reshape(4, SLOT, TILE)

    def send_block(sb, rb, h, rel, copies):
        axis, s = 1 - h, at(h, rel)
        copies[h, rel] = []
        for off in (2, 1, 3):
            cp = sems.remote(
                sb.at[h, at(axis, off), s], rb.at[h, spot[axis], s], peer(axis, off)
            )
            cp.start()
            copies[h, rel].append(cp)

    def keep_own(sb, rb, h, copies):
        axis = 1 - h
        cp = sems.copy(sb.at[h, spot[axis]], rb.at[h, spot[axis]])
        cp.start()
        copies[h] = cp

    def pack_send(way, ag, sb, rb, rel, copies):
        for h in (0, 1):
            pack(way, ag, sb, h, at(h, rel))
            send_block(sb, rb, h, rel, copies)

    def all_sent(copies):
        for h in (0, 1):
            copies[h].wait()
            for rel in range(4):
                for cp in copies[h, rel]:
                    cp.wait_send()

    def all_arrived(copies):
        for h in (0, 1):
            for rel in range(4):
                for cp in copies[h, rel]:
                    cp.wait_recv()

    def received(copies):
        for cp in copies:
            cp.wait_recv()

    def sent(copies):
        for cp in copies:
            cp.wait_send()

    build_onehot(1, 0)
    for cp in meta_x:
        cp.wait()
    build_onehot(1, 1)
    d_xb, d_dy, d_xf = {}, {}, {}
    f_xb = gather_forward(ag_xb, g_xb)
    for rel in (0, 1, 3):
        pack_send(1, ag_xb, sb_0, sl_xb, rel, d_xb)
    f_dy = gather_forward(ag_dy, g_dy)
    received(f_xb)
    pack_send(1, ag_xb, sb_0, sl_xb, 2, d_xb)
    for rel in (0, 1, 3):
        pack_send(1, ag_dy, sb_1, sl_dy, rel, d_dy)
    received(f_dy)
    pack_send(1, ag_dy, sb_1, sl_dy, 2, d_dy)
    g_xf = gather_start(ag_xf)
    for h in (0, 1):
        keep_own(sb_0, sl_xb, h, d_xb)
        keep_own(sb_1, sl_dy, h, d_dy)
    build_onehot(0, 0)
    build_onehot(0, 1)

    def slots_of(sl, h, zi, xi):
        block = sl[h, xi, zi] if h == 0 else sl[h, zi, xi]
        return block.astype(f32)

    def by_expert(sl, h, i, j):
        zi, xi = i // 2, 2 * (i % 2)
        first = slots_of(sl, h, zi, xi)[j * CAP : (j + 1) * CAP]
        second = slots_of(sl, h, zi, xi + 1)[j * CAP : (j + 1) * CAP]
        return jnp.concatenate([first, second], axis=0)

    cap_rows = lax.broadcasted_iota(jnp.int32, (CAP, TOK), 0)

    def normalize(sl, way):
        def one(i):
            zi, xi = i // 2, 2 * (i % 2)
            shift, scale = modulation_of(way, i, 0), modulation_of(way, i, 1)
            for j in (0, 1):
                left, right = by_expert(sl, 0, i, j), by_expert(sl, 1, i, j)
                total = jnp.sum(left, axis=1, keepdims=True) + jnp.sum(right, axis=1, keepdims=True)
                center = total * (1.0 / D)
                left, right = left - center, right - center
                total = jnp.sum(left * left, axis=1, keepdims=True) + jnp.sum(
                    right * right, axis=1, keepdims=True
                )
                inv = lax.rsqrt(total * (1.0 / D) + epsilon)
                for h, part in ((0, left), (1, right)):
                    span = slice(h * HALF, (h + 1) * HALF)
                    mixed = part * inv * (1.0 + scale[:, span]) + shift[:, span]
                    xm[j, i, :, span] = mixed.astype(bf16)
                if way:
                    cols[j, i, :, MU_B] = center
                    cols[j, i, :, ISTD_B] = inv
                ids = (cap_rows + (me * SLOT + j * CAP)).astype(f32)
                found = []
                for par in (0, 1):
                    block = meta[xi + par, zi]
                    s0, s1, e0, e1 = [
                        block[4 * way + k : 4 * way + k + 1, :] for k in range(4)
                    ]
                    hit = jnp.where(ids == s0, e1, 0.0) + jnp.where(ids == s1, e0, 0.0)
                    found.append(jnp.sum(hit, axis=1, keepdims=True))
                cols[j, i, :, OTHER] = jnp.concatenate(found, axis=0)

        loop(IMAGES, one)

    lane = lax.broadcasted_iota(jnp.int32, (ROWS, EXPERTS), 1)

    def picks(j):
        own = (lane == 2 * me + j).astype(f32)
        return own - (lane.astype(f32) == cols[j, :, :, OTHER].reshape(ROWS, 1)).astype(f32)

    def experts_up(keep):
        def one(j):
            rows = xm[j].reshape(ROWS, D)
            logits = dot_nt(rows, router_ref[0])
            gap = jnp.sum(logits * picks(j), axis=1, keepdims=True)
            chance = 1.0 / (1.0 + jnp.exp(-gap))
            cols[j, :, :, PROB] = chance.reshape(IMAGES, SLOT, 1)
            if keep:
                cols[j, :, :, PROB2] = (chance * (1.0 / (1.0 + jnp.exp(gap)))).reshape(IMAGES, SLOT, 1)
            for f0, f1 in FF_TILES:
                part = dot_nt(rows, up[j, f0:f1, :])
                if keep:
                    pre[j, :, f0:f1] = part
                hid[j, :, f0:f1] = gelu(part).astype(bf16)

        loop(2, one)

    def put_rows(sb, h, n):
        def one(i):
            zi, xi = i // 2, 2 * (i % 2)
            a, b = tile_out[0, i], tile_out[1, i]
            for par in (0, 1):
                block = jnp.concatenate(
                    [a[par * CAP : (par + 1) * CAP], b[par * CAP : (par + 1) * CAP]], axis=0
                ).astype(bf16)
                span = slice(n * TILE, (n + 1) * TILE)
                if h == 0:
                    sb[h, xi + par, zi, :, span] = block
                else:
                    sb[h, zi, xi + par, :, span] = block

        loop(IMAGES, one)

    all_arrived(d_xb)
    all_sent(d_xb)
    sent(g_xb + f_xb)
    normalize(sl_xb, 1)
    f_xf = gather_forward(ag_xf, g_xf)
    up_copy.wait()
    experts_up(True)
    down_copy.wait()

    def out_place(j, i):
        return 2 * j + i // 4, i % 4

    for n in range(D // TILE):
        h, inner = n // 2, slice((n % 2) * TILE, (n % 2 + 1) * TILE)

        def out_tile(j):
            part = dot(hid[j], down[j, :, n * TILE : (n + 1) * TILE]).astype(bf16)
            part = part.reshape(2, 4, SLOT, TILE)
            for k in (0, 1):
                sb_0[h, 2 * j + k, :, :, inner] = part[k]

        loop(2, out_tile)

    all_sent(d_dy)
    sent(g_dy + f_dy)
    for rel in (0, 1, 3):
        pack_send(0, ag_xf, sb_1, sl_xf, rel, d_xf)
    received(f_xf)
    pack_send(0, ag_xf, sb_1, sl_xf, 2, d_xf)
    for h in (0, 1):
        keep_own(sb_1, sl_xf, h, d_xf)
    all_arrived(d_dy)

    cols[:, :, :, PGRAD] = jnp.zeros((2, IMAGES, SLOT, 1), f32)

    def out_image(i):
        for h in (0, 1):
            span = slice(h * HALF, (h + 1) * HALF)
            gate = modulation_of(1, i, 2, span)
            total = jnp.zeros((1, HALF), f32)
            for j in (0, 1):
                a, b = out_place(j, i)
                out = sb_0[h, a, b].astype(f32)
                dyv = by_expert(sl_dy, h, i, j)
                chance = cols[j, i, :, PROB]
                mix = (dyv * gate).astype(bf16).astype(f32)
                cols[j, i, :, PGRAD] += jnp.sum(out * mix, axis=1, keepdims=True)
                total += jnp.sum(out * dyv * chance, axis=0, keepdims=True)
                og[j, i, :, span] = (chance.astype(bf16).astype(f32) * mix).astype(bf16)
            stat[2, pl.ds(i, 1), span] = total

    loop(IMAGES, out_image)

    def hidden_grad(j):
        rows = og[j].reshape(ROWS, D)
        for f0, f1 in FF_TILES:
            part = dot_nt(rows, down[j, f0:f1, :])
            pgr[j, :, f0:f1] = (part * gelu_slope(pre[j, :, f0:f1])).astype(bf16)
        weight = picks(j) * (cols[j, :, :, PGRAD] * cols[j, :, :, PROB2]).reshape(ROWS, 1)
        high = weight.astype(bf16)
        wrow[j, 0] = high
        wrow[j, 1] = (weight - high.astype(f32)).astype(bf16)

    loop(2, hidden_grad)
    r_b, r_f = {}, {}
    for n in range(D // TILE):
        span = slice(n * TILE, (n + 1) * TILE)

        def grad_tile(j):
            part = dot(pgr[j], up[j, :, span]).astype(bf16).astype(f32)
            rows = router_ref[0, :, span]
            part += dot(wrow[j, 0], rows) + dot(wrow[j, 1], rows)
            tile_out[j] = part.reshape(IMAGES, SLOT, TILE)

        loop(2, grad_tile)
        put_rows(sb_0, n // 2, n % 2)
        if n % 2:
            for rel in (2, 1, 3, 0):
                send_block(sb_0, rr_b, n // 2, rel, r_b)
            keep_own(sb_0, rr_b, n // 2, r_b)

    kept = []
    for source, dest in ((xm, xm_out), (og, og_out), (hid, hid_out), (pgr, pg_out)):
        cp = sems.copy(source, dest)
        cp.start()
        kept.append(cp)

    for n in range(D // TILE):
        span = slice(n * TILE, (n + 1) * TILE)
        rg = jnp.zeros((EXPERTS, TILE), f32)
        for j in (0, 1):
            block = xm[j, :, :, span].reshape(ROWS, TILE)
            rg += dot_tn(wrow[j, 0], block) + dot_tn(wrow[j, 1], block)
        for k in range(EXPERTS // 8):
            stat[3 + k, :, span] = rg[8 * k : 8 * k + 8]

    all_arrived(d_xf)
    all_sent(d_xf)
    sent(g_xf + f_xf)
    for cp in kept:
        cp.wait()
    normalize(sl_xf, 0)
    experts_up(False)
    for n in range(D // TILE):
        span = slice(n * TILE, (n + 1) * TILE)

        def give_tile(j):
            part = dot(hid[j], down[j, :, span]) * cols[j, :, :, PROB].reshape(ROWS, 1)
            tile_out[j] = part.reshape(IMAGES, SLOT, TILE)

        loop(2, give_tile)
        put_rows(sb_1, n // 2, n % 2)
        if n % 2:
            for rel in (2, 1, 3, 0):
                send_block(sb_1, rr_f, n // 2, rel, r_f)
            keep_own(sb_1, rr_f, n // 2, r_f)

    def summed(way, rr, h, s):
        block = rr[h, :, s]
        return dot_tn(onehot[way, h, s], block.reshape(4 * SLOT, HALF))

    def return_far(way, rr, ag, hop, arriving):
        copies = []
        for h in (0, 1):
            arriving[h].wait()
            received(arriving[h, 2])
            s = at(h, 2)
            ag[h, s] = summed(way, rr, h, s).astype(bf16)
            for k, off in enumerate((1, 3)):
                cp = sems.remote(ag.at[h, s, pl.ds(64 * k, 64)], hop.at[h, k], peer(h, off))
                cp.start()
                copies.append(cp)
        return copies

    def return_near(way, rr, ag, hop, last, arriving, far):
        copies = []
        for h in (0, 1):
            for k, off in enumerate((1, 3)):
                received(arriving[h, off])
                s = at(h, off)
                part = summed(way, rr, h, s)
                far[2 * h + k].wait_recv()
                rows = slice(64 * k, 64 * k + 64)
                rest = slice(64 * (1 - k), 64 * (1 - k) + 64)
                ag[h, s, rest] = part[rest].astype(bf16)
                ag[h, s, rows] = (part[rows] + hop[h, k].astype(f32)).astype(bf16)
                cp = sems.remote(ag.at[h, s], last.at[h, k], peer(h, off))
                cp.start()
                copies.append(cp)
        return copies

    def return_own(way, rr, arriving):
        for h in (0, 1):
            received(arriving[h, 0])
            own[h] = summed(way, rr, h, spot[h])

    def total_of(last, near):
        for h in (0, 1):
            received(near[2 * h : 2 * h + 2])
            own[h] += last[h, 0].astype(f32) + last[h, 1].astype(f32)

    far_b = return_far(1, rr_b, ag_xb, hop_b, r_b)

    def grad_image(i):
        zi, xi = i // 2, 2 * (i % 2)
        for h in (0, 1):
            span = slice(h * HALF, (h + 1) * HALF)
            shift = jnp.zeros((1, HALF), f32)
            scale = jnp.zeros((1, HALF), f32)
            for par in (0, 1):
                cut = slice(par * CAP, (par + 1) * CAP)
                center, inv = [
                    jnp.concatenate([cols[0, i, cut, k], cols[1, i, cut, k]], axis=0)
                    for k in (MU_B, ISTD_B)
                ]
                grad = slots_of(sb_0, h, zi, xi + par)
                normed = (slots_of(sl_xb, h, zi, xi + par) - center) * inv
                shift += jnp.sum(grad, axis=0, keepdims=True)
                scale += jnp.sum(grad * normed, axis=0, keepdims=True)
            stat[0, pl.ds(i, 1), span] = shift
            stat[1, pl.ds(i, 1), span] = scale

    loop(IMAGES, grad_image)
    sum_z = [
        sems.remote(
            stat.at[:, :, pl.ds(pl.multiple_of(at(0, off) * TILE, TILE), TILE)],
            st_z.at[z],
            peer(0, off),
        )
        for off in (1, 2, 3)
    ]
    for cp in sum_z:
        cp.start()
    near_b = return_near(1, rr_b, ag_xb, hop_b, last_b, r_b, far_b)
    return_own(1, rr_b, r_b)

    for cp in sum_z:
        cp.wait()
    st_z[z] = stat[:, :, pl.ds(pl.multiple_of(z * TILE, TILE), TILE)]
    st_2[...] = st_z[0] + st_z[1] + st_z[2] + st_z[3]
    sum_x = [
        sems.remote(
            st_2.at[:, :, pl.ds(pl.multiple_of(at(1, off) * TOK, TOK), TOK)],
            st_x.at[x],
            peer(1, off),
        )
        for off in (1, 2, 3)
    ]
    for cp in sum_x:
        cp.start()

    far_f = return_far(0, rr_f, ag_xf, hop_f, r_f)
    for cp in sum_x:
        cp.wait()
    st_x[x] = st_2[:, :, pl.ds(pl.multiple_of(x * TOK, TOK), TOK)]
    own_part = fin.at[:, :, pl.ds(pl.multiple_of(me * TOK, TOK), TOK)]
    own_part[...] = st_x[0] + st_x[1] + st_x[2] + st_x[3]
    give_x = [sems.remote(own_part, own_part, peer(1, off)) for off in (1, 2, 3)]
    for cp in give_x:
        cp.start()

    total_of(last_b, near_b)
    own_scale = modulation_of(1, me // 2, 1)

    def input_grads(c):
        at_rows = pl.ds(pl.multiple_of(c * 32, 32), 32)
        parts = []
        for h in (0, 1):
            parts.append(ag_xb[h, spot[h], at_rows].astype(f32))
        total = jnp.sum(parts[0], axis=1, keepdims=True) + jnp.sum(parts[1], axis=1, keepdims=True)
        center = total * (1.0 / D)
        parts = [part - center for part in parts]
        total = jnp.sum(parts[0] * parts[0], axis=1, keepdims=True) + jnp.sum(
            parts[1] * parts[1], axis=1, keepdims=True
        )
        inv = lax.rsqrt(total * (1.0 / D) + epsilon)
        normed = [part * inv for part in parts]
        grads = []
        for h in (0, 1):
            span = slice(h * HALF, (h + 1) * HALF)
            grads.append(own[h, at_rows] * (1.0 + own_scale[:, span]))
        mean = (
            jnp.sum(grads[0], axis=1, keepdims=True) + jnp.sum(grads[1], axis=1, keepdims=True)
        ) * (1.0 / D)
        slope = (
            jnp.sum(grads[0] * normed[0], axis=1, keepdims=True)
            + jnp.sum(grads[1] * normed[1], axis=1, keepdims=True)
        ) * (1.0 / D)
        for h in (0, 1):
            span = slice(h * HALF, (h + 1) * HALF)
            dyv = ag_dy[h, spot[h], at_rows].astype(f32)
            part = dyv + inv * (grads[h] - mean - normed[h] * slope)
            res[at_rows, span] = part.astype(bf16)

    loop(4, input_grads)
    back_copy = sems.copy(res, out_b)
    back_copy.start()

    near_f = return_near(0, rr_f, ag_xf, hop_f, last_f, r_f, far_f)
    for cp in give_x:
        cp.wait()
    own_part = fin.at[:, :, pl.ds(pl.multiple_of(z * TILE, TILE), TILE)]
    give_z = [sems.remote(own_part, own_part, peer(0, off)) for off in (1, 2, 3)]
    for cp in give_z:
        cp.start()
    return_own(0, rr_f, r_f)
    total_of(last_f, near_f)
    back_copy.wait()
    own_gate = modulation_of(0, me // 2, 2)

    def outputs(c):
        at_rows = pl.ds(pl.multiple_of(c * 32, 32), 32)
        for h in (0, 1):
            span = slice(h * HALF, (h + 1) * HALF)
            part = ag_xf[h, spot[h], at_rows].astype(f32) + own_gate[:, span] * own[h, at_rows]
            res[at_rows, span] = part.astype(bf16)

    loop(4, outputs)
    front_copy = sems.copy(res, out_f)
    front_copy.start()
    for cp in give_z:
        cp.wait()
    fin_copy = sems.copy(fin, fin_out)
    fin_copy.start()
    for copies in (r_b, r_f):
        for h in (0, 1):
            for rel in range(4):
                sent(copies[h, rel])
    sent(far_b + near_b + far_f + near_f)
    front_copy.wait()
    fin_copy.wait()


def layer(routes_f, routes_b, times_f, times_b, table, router, xf, xb, dy, up, down):
    any_spec = pl.BlockSpec(memory_space=pl.ANY)
    vmem = pl.BlockSpec(memory_space=pltpu.VMEM)
    smem = pl.BlockSpec(memory_space=pltpu.SMEM)
    shape = jax.ShapeDtypeStruct
    gather = pltpu.VMEM((2, 4, TOK, HALF), bf16)
    slots = pltpu.VMEM((2, 4, 4, SLOT, HALF), bf16)
    return pl.pallas_call(
        layer_kernel,
        out_shape=(
            shape((TOK, D), bf16),
            shape((TOK, D), bf16),
            shape((2, IMAGES, SLOT, D), bf16),
            shape((2, IMAGES, SLOT, D), bf16),
            shape((2, ROWS, FF), bf16),
            shape((2, ROWS, FF), bf16),
            shape((7, 8, D), f32),
        ),
        in_specs=[vmem, vmem, smem, smem, vmem, vmem] + [any_spec] * 5,
        out_specs=tuple([any_spec] * 7),
        scratch_shapes=[
            pltpu.SemaphoreType.DMA((N_REMOTE,)),
            pltpu.SemaphoreType.DMA((N_REMOTE,)),
            pltpu.SemaphoreType.DMA((N_LOCAL,)),
            pltpu.VMEM((4, 4, 8, TOK), f32),
            pltpu.VMEM((2, 2, 4, 4 * SLOT, TOK), bf16),
            gather,
            gather,
            gather,
            slots,
            slots,
            slots,
            slots,
            slots,
            slots,
            slots,
            pltpu.VMEM((2, 2, 64, HALF), bf16),
            pltpu.VMEM((2, 2, 64, HALF), bf16),
            pltpu.VMEM((2, 2, TOK, HALF), bf16),
            pltpu.VMEM((2, 2, TOK, HALF), bf16),
            pltpu.VMEM((2, TOK, HALF), f32),
            pltpu.VMEM((2, FF, D), bf16),
            pltpu.VMEM((2, FF, D), bf16),
            pltpu.VMEM((2, IMAGES, SLOT, D), bf16),
            pltpu.VMEM((2, IMAGES, SLOT, D), bf16),
            pltpu.VMEM((2, ROWS, FF), f32),
            pltpu.VMEM((2, ROWS, FF), bf16),
            pltpu.VMEM((2, ROWS, FF), bf16),
            pltpu.VMEM((2, IMAGES, SLOT, TILE), f32),
            pltpu.VMEM((3, 2 * IMAGES, D), f32),
            pltpu.VMEM((2, IMAGES, SLOT, 8), f32),
            pltpu.VMEM((2, 2, ROWS, EXPERTS), bf16),
            pltpu.VMEM((7, 8, D), f32),
            pltpu.VMEM((4, 7, 8, TILE), f32),
            pltpu.VMEM((7, 8, TILE), f32),
            pltpu.VMEM((4, 7, 8, TOK), f32),
            pltpu.VMEM((7, 8, D), f32),
            pltpu.VMEM((TOK, D), bf16),
        ],
        compiler_params=pltpu.CompilerParams(
            collective_id=0, has_side_effects=True, vmem_limit_bytes=63 << 20
        ),
        cost_estimate=pl.CostEstimate(
            flops=13_000_000_000, bytes_accessed=30_000_000, transcendentals=2_000_000
        ),
        name="moe_layer",
    )(routes_f, routes_b, times_f, times_b, table, router, xf, xb, dy, up, down)


def gradients_kernel(times, pg, hid, xm, og, sums, up_out, down_out, router_out, table_out, pg_t, hid_t):
    n = pl.program_id(1)

    @pl.when(n == 0)
    def _():
        pg_t[...] = pg[0].T
        hid_t[...] = hid[0].T

    up_out[0, 0] = dot(pg_t[...], xm[0]).astype(bf16)
    down_out[0, 0] = dot(hid_t[...], og[0]).astype(bf16)

    @pl.when((n == 0) & (pl.program_id(0) == 0))
    def _():
        for k in range(EXPERTS // 8):
            router_out[0, 8 * k : 8 * k + 8] = sums[3 + k]
        steps = lax.broadcasted_iota(jnp.int32, (16, 1), 0)
        for c in range(3):
            total = jnp.zeros((16, D), f32)
            for i in range(IMAGES):
                total += jnp.where(steps == times[0, i], sums[c, i : i + 1, :], 0.0)
            table_out[0, c] = total


def gradients(times, pg, hid, xm, og, sums):
    shape = jax.ShapeDtypeStruct
    whole = lambda j, n: (j, 0, 0)
    part = lambda j, n: (j, 0, n)
    return pl.pallas_call(
        gradients_kernel,
        grid=(2, D // TILE),
        out_shape=(
            shape((1, 2, FF, D), bf16),
            shape((1, 2, FF, D), bf16),
            shape((1, EXPERTS, D), f32),
            shape((1, 3, 16, D), f32),
        ),
        in_specs=[
            pl.BlockSpec(memory_space=pltpu.SMEM),
            pl.BlockSpec((1, ROWS, FF), whole),
            pl.BlockSpec((1, ROWS, FF), whole),
            pl.BlockSpec((1, ROWS, TILE), part),
            pl.BlockSpec((1, ROWS, TILE), part),
            pl.BlockSpec((7, 8, D), lambda j, n: (0, 0, 0)),
        ],
        out_specs=(
            pl.BlockSpec((1, 1, FF, TILE), lambda j, n: (0, j, 0, n)),
            pl.BlockSpec((1, 1, FF, TILE), lambda j, n: (0, j, 0, n)),
            pl.BlockSpec((1, EXPERTS, D), lambda j, n: (0, 0, 0)),
            pl.BlockSpec((1, 3, 16, D), lambda j, n: (0, 0, 0, 0)),
        ),
        scratch_shapes=[pltpu.VMEM((FF, ROWS), bf16), pltpu.VMEM((FF, ROWS), bf16)],
        compiler_params=pltpu.CompilerParams(vmem_limit_bytes=60 << 20),
        cost_estimate=pl.CostEstimate(
            flops=4_500_000_000, bytes_accessed=22_000_000, transcendentals=0
        ),
        name="weight_grads",
    )(times, pg, hid, xm, og, sums)


def passed_along(value, steps):
    count = lax.axis_size("section")
    pairs = [(source, (source + steps) % count) for source in range(count)]
    return lax.ppermute(value, "section", pairs)


def per_device(
    forward_input,
    backward_input,
    backward_grad,
    forward_routes,
    backward_routes,
    forward_times,
    backward_times,
    modulation,
    router_weight,
    expert_up,
    expert_down,
):
    block_out, input_part, rows, out_grad, hidden, pre_grad, sums = layer(
        forward_routes[0].T,
        backward_routes[0].T,
        forward_times,
        backward_times,
        modulation.transpose(0, 2, 1, 3),
        router_weight.transpose(0, 2, 1),
        forward_input,
        backward_input,
        backward_grad,
        expert_up.transpose(0, 1, 3, 2),
        expert_down,
    )
    input_grad = passed_along(input_part, -1)
    forward_output = passed_along(block_out, 1)
    rows = rows.reshape(2, ROWS, D)
    out_grad = out_grad.reshape(2, ROWS, D)
    up_grad, down_grad, router_grad, table_grad = gradients(
        backward_times, pre_grad, hidden, rows, out_grad, sums
    )
    return (
        forward_output[None],
        input_grad[None],
        up_grad.transpose(0, 1, 3, 2),
        down_grad,
        router_grad.transpose(0, 2, 1),
        table_grad.transpose(0, 2, 1, 3),
    )


def solution(mesh):
    placed = (
        P("section", "ep", None),
        P("section", "ep", None),
        P("section", "ep", None),
        P("section", "ep", None),
        P("section", "ep", None),
        P("section", None),
        P("section", None),
        P("section", None, None, None),
        P("section", None, None),
        P("section", "ep", None, None),
        P("section", "ep", None, None),
    )
    return jax.shard_map(
        per_device,
        mesh=mesh,
        in_specs=placed,
        out_specs=(
            P("section", "ep", None),
            P("section", "ep", None),
            P("section", "ep", None, None),
            P("section", "ep", None, None),
            P("section", None, None),
            P("section", None, None, None),
        ),
        check_vma=False,
    )
```

```python
import jax
import jax.numpy as jnp
from jax import lax
from jax.experimental import pallas as pl
from jax.experimental.pallas import tpu as pltpu
from jax.sharding import PartitionSpec as P

D = 2048
HALF = 1024
FF = 704
TOK = 128
CAP = 24
SLOT = 2 * CAP
EXPERTS = 32
IMAGES = 8
ROWS = IMAGES * SLOT
STAT = 56
TILE = 512
epsilon = 1e-06
MESH = pl.DeviceIdType.MESH
f32 = jnp.float32
bf16 = jnp.bfloat16
FF_TILES = ((0, 256), (256, 512), (512, 704))
PROB, PROB2, OTHER, PGRAD, MU_B, ISTD_B = (slice(k, k + 1) for k in range(6))
GELU_A = 0.7978845608028654
GELU_B = 0.044715


def dot(a, b):
    return jnp.dot(a, b, preferred_element_type=f32)


def dot_nt(a, b):
    return lax.dot_general(a, b, (((1,), (1,)), ((), ())), preferred_element_type=f32)


def dot_tn(a, b):
    return lax.dot_general(a, b, (((0,), (0,)), ((), ())), preferred_element_type=f32)


def gelu(values):
    inner = jnp.tanh(GELU_A * (values + GELU_B * values * values * values))
    return 0.5 * values * (1.0 + inner)


def gelu_slope(values):
    square = values * values
    inner = jnp.tanh(GELU_A * (values + GELU_B * values * square))
    outer = 0.5 * values * (1.0 - inner * inner) * (GELU_A * (1.0 + 3.0 * GELU_B * square))
    return 0.5 * (1.0 + inner) + outer


def loop(count, body):
    def step(index, carry):
        body(index)
        return carry

    lax.fori_loop(0, count, step, 0)


class Sems:
    def __init__(self, send, recv, local):
        self.send, self.recv, self.local = send, recv, local
        self.remote_used = self.local_used = 0

    def remote(self, src, dst, device):
        k = self.remote_used
        self.remote_used += 1
        return pltpu.make_async_remote_copy(
            src_ref=src,
            dst_ref=dst,
            send_sem=self.send.at[k],
            recv_sem=self.recv.at[k],
            device_id=device,
            device_id_type=MESH,
        )

    def copy(self, src, dst):
        k = self.local_used
        self.local_used += 1
        return pltpu.make_async_copy(src, dst, self.local.at[k])


N_REMOTE = 200
N_LOCAL = 40


def layer_kernel(
    routes_f,
    routes_b,
    times_f,
    times_b,
    table_ref,
    router_ref,
    xf_hbm,
    xb_hbm,
    dy_hbm,
    up_hbm,
    down_hbm,
    out_f,
    out_b,
    xm_out,
    og_out,
    hid_out,
    pg_out,
    fin_out,
    send_sem,
    recv_sem,
    local_sem,
    meta,
    onehot,
    ag_xb,
    ag_dy,
    ag_xf,
    sb_0,
    sb_1,
    sl_xb,
    sl_dy,
    sl_xf,
    rr_b,
    rr_f,
    hop_b,
    hop_f,
    last_b,
    last_f,
    own,
    up,
    down,
    xm,
    og,
    pre,
    hid,
    pgr,
    tile_out,
    modr,
    cols,
    wrow,
    stat,
    st_z,
    st_2,
    st_x,
    fin,
    res,
):
    section = lax.axis_index("section")
    me = lax.axis_index("ep")
    z, x = me // 4, me % 4
    sems = Sems(send_sem, recv_sem, local_sem)

    def peer(axis, off):
        if axis == 0:
            return (section, lax.rem(z + off + 4, 4) * 4 + x)
        return (section, z * 4 + lax.rem(x + off + 4, 4))

    spot = (z, x)

    def at(axis, off):
        return lax.rem(spot[axis] + off + 4, 4)

    barrier = pltpu.get_barrier_semaphore()
    for axis in (0, 1):
        for off in (1, 2, 3):
            pl.semaphore_signal(barrier, inc=1, device_id=peer(axis, off), device_id_type=MESH)

    own_copies = []
    for source, ag in ((xb_hbm, ag_xb), (dy_hbm, ag_dy), (xf_hbm, ag_xf)):
        for h in (0, 1):
            cp = sems.copy(source.at[0, :, pl.ds(h * HALF, HALF)], ag.at[h, spot[h]])
            cp.start()
            own_copies.append(cp)
    up_copy = sems.copy(up_hbm.at[0], up)
    down_copy = sems.copy(down_hbm.at[0], down)

    expert_rows = lax.broadcasted_iota(jnp.int32, (EXPERTS, TOK), 0).astype(f32)
    earlier = (
        lax.broadcasted_iota(jnp.int32, (TOK, TOK), 0)
        < lax.broadcasted_iota(jnp.int32, (TOK, TOK), 1)
    ).astype(bf16)
    for way in (0, 1):
        routes = routes_b if way else routes_f
        e0 = routes[0:1, :].astype(f32)
        e1 = routes[1:2, :].astype(f32)
        o0 = (expert_rows == e0).astype(f32)
        o1 = (expert_rows == e1).astype(f32)
        rank = dot((o0 + o1).astype(bf16), earlier)
        s0 = e0 * CAP + jnp.sum(o0 * rank, axis=0, keepdims=True)
        s1 = e1 * CAP + jnp.sum(o1 * rank, axis=0, keepdims=True)
        for k, row in enumerate((s0, s1, e0, e1)):
            meta[x, z, 4 * way + k : 4 * way + k + 1, :] = row

    pl.semaphore_wait(barrier, 6)

    meta_z = [sems.remote(meta.at[x, z], meta.at[x, z], peer(0, off)) for off in (1, 2, 3)]
    for cp in meta_z:
        cp.start()

    def gather_start(ag):
        copies = []
        for off in (1, 3):
            for h in (0, 1):
                block = ag.at[h, spot[h]]
                cp = sems.remote(block, block, peer(h, off))
                cp.start()
                copies.append(cp)
        return copies

    def gather_forward(ag, first):
        copies = []
        for k, off in enumerate((1, 3)):
            for h in (0, 1):
                first[2 * k + h].wait_recv()
                block = ag.at[h, at(h, -off), pl.ds(64 * k, 64)]
                cp = sems.remote(block, block, peer(h, off))
                cp.start()
                copies.append(cp)
        return copies

    for cp in own_copies[0:2]:
        cp.wait()
    g_xb = gather_start(ag_xb)

    time_rows = lax.broadcasted_iota(jnp.int32, (2 * IMAGES, 16), 0)
    time_of = jnp.zeros((2 * IMAGES, 16), jnp.int32)
    for i in range(IMAGES):
        time_of = jnp.where(time_rows == i, times_f[0, i], time_of)
        time_of = jnp.where(time_rows == IMAGES + i, times_b[0, i], time_of)
    chosen = (time_of == lax.broadcasted_iota(jnp.int32, (2 * IMAGES, 16), 1)).astype(f32)
    for c in range(3):
        modr[c] = dot(chosen.astype(bf16), table_ref[0, c])

    def modulation_of(way, i, c, span=slice(0, D)):
        return modr[c, pl.ds(i + IMAGES * way, 1), span]

    for cp in meta_z:
        cp.wait()
    meta_x = [sems.remote(meta.at[x], meta.at[x], peer(1, off)) for off in (1, 2, 3)]
    for cp in meta_x:
        cp.start()
    for cp in own_copies[2:4]:
        cp.wait()
    g_dy = gather_start(ag_dy)

    slot_rows = lax.broadcasted_iota(jnp.int32, (4 * SLOT, TOK), 0)

    def build_onehot(way, h):
        if h == 0:
            ids = slot_rows + z * 192
        else:
            block = (
                (slot_rows >= 48).astype(jnp.int32)
                + (slot_rows >= 96).astype(jnp.int32)
                + (slot_rows >= 144).astype(jnp.int32)
            )
            ids = slot_rows + block * 144 + x * SLOT
        ids = ids.astype(f32)

        def one(s):
            block = meta[x, s] if h == 0 else meta[s, z]
            s0 = block[4 * way : 4 * way + 1, :]
            s1 = block[4 * way + 1 : 4 * way + 2, :]
            onehot[way, h, s] = ((ids == s0).astype(f32) + (ids == s1).astype(f32)).astype(bf16)

        loop(4, one)

    def pack(way, ag, sb, h, s):
        for n in (0, 1):
            part = dot(onehot[way, h, s], ag[h, s, :, n * TILE : (n + 1) * TILE])
            sb[h, :, s, :, n * TILE : (n + 1) * TILE] = part.astype(bf16).reshape(4, SLOT, TILE)

    def send_block(sb, rb, h, rel, copies):
        axis, s = 1 - h, at(h, rel)
        copies[h, rel] = []
        for off in (2, 1, 3):
            cp = sems.remote(
                sb.at[h, at(axis, off), s], rb.at[h, spot[axis], s], peer(axis, off)
            )
            cp.start()
            copies[h, rel].append(cp)

    def keep_own(sb, rb, h, copies):
        axis = 1 - h
        cp = sems.copy(sb.at[h, spot[axis]], rb.at[h, spot[axis]])
        cp.start()
        copies[h] = cp

    def pack_send(way, ag, sb, rb, rel, copies):
        for h in (0, 1):
            pack(way, ag, sb, h, at(h, rel))
            send_block(sb, rb, h, rel, copies)

    def all_sent(copies):
        for h in (0, 1):
            copies[h].wait()
            for rel in range(4):
                for cp in copies[h, rel]:
                    cp.wait_send()

    def all_arrived(copies):
        for h in (0, 1):
            for rel in range(4):
                for cp in copies[h, rel]:
                    cp.wait_recv()

    def received(copies):
        for cp in copies:
            cp.wait_recv()

    def sent(copies):
        for cp in copies:
            cp.wait_send()

    d_xb, d_dy, d_xf = {}, {}, {}
    build_onehot(1, 0)
    f_xb = gather_forward(ag_xb, g_xb)
    for h in (0, 1):
        if h:
            for cp in meta_x:
                cp.wait()
            build_onehot(1, 1)
        for rel in (0, 1, 3):
            pack(1, ag_xb, sb_0, h, at(h, rel))
            send_block(sb_0, sl_xb, h, rel, d_xb)
    f_dy = gather_forward(ag_dy, g_dy)
    received(f_xb)
    pack_send(1, ag_xb, sb_0, sl_xb, 2, d_xb)
    for rel in (0, 1, 3):
        pack_send(1, ag_dy, sb_1, sl_dy, rel, d_dy)
    for cp in own_copies[4:6]:
        cp.wait()
    g_xf = gather_start(ag_xf)
    received(f_dy)
    pack_send(1, ag_dy, sb_1, sl_dy, 2, d_dy)
    up_copy.start()
    down_copy.start()
    for h in (0, 1):
        keep_own(sb_0, sl_xb, h, d_xb)
        keep_own(sb_1, sl_dy, h, d_dy)
    build_onehot(0, 0)
    build_onehot(0, 1)

    def slots_of(sl, h, zi, xi):
        block = sl[h, xi, zi] if h == 0 else sl[h, zi, xi]
        return block.astype(f32)

    def by_expert(sl, h, i, j):
        zi, xi = i // 2, 2 * (i % 2)
        first = slots_of(sl, h, zi, xi)[j * CAP : (j + 1) * CAP]
        second = slots_of(sl, h, zi, xi + 1)[j * CAP : (j + 1) * CAP]
        return jnp.concatenate([first, second], axis=0)

    cap_rows = lax.broadcasted_iota(jnp.int32, (CAP, TOK), 0)

    def normalize(sl, way):
        def one(i):
            zi, xi = i // 2, 2 * (i % 2)
            shift, scale = modulation_of(way, i, 0), modulation_of(way, i, 1)
            for j in (0, 1):
                left, right = by_expert(sl, 0, i, j), by_expert(sl, 1, i, j)
                total = jnp.sum(left, axis=1, keepdims=True) + jnp.sum(right, axis=1, keepdims=True)
                center = total * (1.0 / D)
                left, right = left - center, right - center
                total = jnp.sum(left * left, axis=1, keepdims=True) + jnp.sum(
                    right * right, axis=1, keepdims=True
                )
                inv = lax.rsqrt(total * (1.0 / D) + epsilon)
                for h, part in ((0, left), (1, right)):
                    span = slice(h * HALF, (h + 1) * HALF)
                    mixed = part * inv * (1.0 + scale[:, span]) + shift[:, span]
                    xm[j, i, :, span] = mixed.astype(bf16)
                if way:
                    cols[j, i, :, MU_B] = center
                    cols[j, i, :, ISTD_B] = inv
                ids = (cap_rows + (me * SLOT + j * CAP)).astype(f32)
                found = []
                for par in (0, 1):
                    block = meta[xi + par, zi]
                    s0, s1, e0, e1 = [
                        block[4 * way + k : 4 * way + k + 1, :] for k in range(4)
                    ]
                    hit = jnp.where(ids == s0, e1, 0.0) + jnp.where(ids == s1, e0, 0.0)
                    found.append(jnp.sum(hit, axis=1, keepdims=True))
                cols[j, i, :, OTHER] = jnp.concatenate(found, axis=0)

        loop(IMAGES, one)

    lane = lax.broadcasted_iota(jnp.int32, (ROWS, EXPERTS), 1)

    def picks(j):
        own = (lane == 2 * me + j).astype(f32)
        return own - (lane.astype(f32) == cols[j, :, :, OTHER].reshape(ROWS, 1)).astype(f32)

    def experts_up(keep):
        def one(j):
            rows = xm[j].reshape(ROWS, D)
            logits = dot_nt(rows, router_ref[0])
            gap = jnp.sum(logits * picks(j), axis=1, keepdims=True)
            chance = 1.0 / (1.0 + jnp.exp(-gap))
            cols[j, :, :, PROB] = chance.reshape(IMAGES, SLOT, 1)
            if keep:
                cols[j, :, :, PROB2] = (chance * (1.0 / (1.0 + jnp.exp(gap)))).reshape(IMAGES, SLOT, 1)
            for f0, f1 in FF_TILES:
                part = dot_nt(rows, up[j, f0:f1, :])
                if keep:
                    pre[j, :, f0:f1] = part
                hid[j, :, f0:f1] = gelu(part).astype(bf16)

        loop(2, one)

    def put_rows(sb, h, n):
        def one(i):
            zi, xi = i // 2, 2 * (i % 2)
            a, b = tile_out[0, i], tile_out[1, i]
            for par in (0, 1):
                block = jnp.concatenate(
                    [a[par * CAP : (par + 1) * CAP], b[par * CAP : (par + 1) * CAP]], axis=0
                ).astype(bf16)
                span = slice(n * TILE, (n + 1) * TILE)
                if h == 0:
                    sb[h, xi + par, zi, :, span] = block
                else:
                    sb[h, zi, xi + par, :, span] = block

        loop(IMAGES, one)

    all_arrived(d_xb)
    all_sent(d_xb)
    sent(g_xb + f_xb)
    normalize(sl_xb, 1)
    f_xf = gather_forward(ag_xf, g_xf)
    up_copy.wait()
    experts_up(True)
    kept = [sems.copy(xm, xm_out), sems.copy(hid, hid_out)]
    for cp in kept:
        cp.start()
    down_copy.wait()

    for n in range(D // TILE):
        span = slice(n * TILE, (n + 1) * TILE)

        def out_tile(j):
            part = dot(hid[j], down[j, :, span]).astype(bf16)
            og[j, :, :, span] = part.reshape(IMAGES, SLOT, TILE)

        loop(2, out_tile)

    for h in (0, 1):
        for rel in (0, 1, 3):
            pack(0, ag_xf, sb_0, h, at(h, rel))
    for rel in (0, 1, 3):
        for h in (0, 1):
            sent(d_dy[h, rel])
    for rel in (0, 1, 3):
        for h in (0, 1):
            send_block(sb_0, sl_xf, h, rel, d_xf)
    received(f_xf)
    pack_send(0, ag_xf, sb_0, sl_xf, 2, d_xf)
    for h in (0, 1):
        keep_own(sb_0, sl_xf, h, d_xf)
    all_arrived(d_dy)
    for h in (0, 1):
        d_dy[h].wait()
        sent(d_dy[h, 2])
    sent(g_dy + f_dy)

    cols[:, :, :, PGRAD] = jnp.zeros((2, IMAGES, SLOT, 1), f32)

    def out_image(i):
        for h in (0, 1):
            span = slice(h * HALF, (h + 1) * HALF)
            gate = modulation_of(1, i, 2, span)
            total = jnp.zeros((1, HALF), f32)
            for j in (0, 1):
                out = og[j, i, :, span].astype(f32)
                dyv = by_expert(sl_dy, h, i, j)
                chance = cols[j, i, :, PROB]
                mix = (dyv * gate).astype(bf16).astype(f32)
                cols[j, i, :, PGRAD] += jnp.sum(out * mix, axis=1, keepdims=True)
                total += jnp.sum(out * dyv * chance, axis=0, keepdims=True)
                og[j, i, :, span] = (chance.astype(bf16).astype(f32) * mix).astype(bf16)
            stat[2, pl.ds(i, 1), span] = total

    loop(IMAGES, out_image)

    def hidden_grad(j):
        rows = og[j].reshape(ROWS, D)
        for f0, f1 in FF_TILES:
            part = dot_nt(rows, down[j, f0:f1, :])
            pgr[j, :, f0:f1] = (part * gelu_slope(pre[j, :, f0:f1])).astype(bf16)
        weight = picks(j) * (cols[j, :, :, PGRAD] * cols[j, :, :, PROB2]).reshape(ROWS, 1)
        high = weight.astype(bf16)
        wrow[j, 0] = high
        wrow[j, 1] = (weight - high.astype(f32)).astype(bf16)

    loop(2, hidden_grad)
    r_b, r_f = {}, {}
    for n in range(D // TILE):
        span = slice(n * TILE, (n + 1) * TILE)

        def grad_tile(j):
            part = dot(pgr[j], up[j, :, span]).astype(bf16).astype(f32)
            rows = router_ref[0, :, span]
            part += dot(wrow[j, 0], rows) + dot(wrow[j, 1], rows)
            tile_out[j] = part.reshape(IMAGES, SLOT, TILE)

        loop(2, grad_tile)
        put_rows(sb_1, n // 2, n % 2)
        if n % 2:
            for rel in (2, 1, 3, 0):
                send_block(sb_1, rr_b, n // 2, rel, r_b)
            keep_own(sb_1, rr_b, n // 2, r_b)

    kept_late = [sems.copy(og, og_out), sems.copy(pgr, pg_out)]
    for cp in kept_late:
        cp.start()

    for n in range(D // TILE):
        span = slice(n * TILE, (n + 1) * TILE)
        rg = jnp.zeros((EXPERTS, TILE), f32)
        for j in (0, 1):
            block = xm[j, :, :, span].reshape(ROWS, TILE)
            rg += dot_tn(wrow[j, 0], block) + dot_tn(wrow[j, 1], block)
        for k in range(EXPERTS // 8):
            stat[3 + k, :, span] = rg[8 * k : 8 * k + 8]

    all_arrived(d_xf)
    all_sent(d_xf)
    sent(g_xf + f_xf)
    for cp in kept:
        cp.wait()
    normalize(sl_xf, 0)
    experts_up(False)
    for n in range(D // TILE):
        span = slice(n * TILE, (n + 1) * TILE)

        def give_tile(j):
            part = dot(hid[j], down[j, :, span]) * cols[j, :, :, PROB].reshape(ROWS, 1)
            tile_out[j] = part.reshape(IMAGES, SLOT, TILE)

        loop(2, give_tile)
        put_rows(sb_0, n // 2, n % 2)
        if n % 2:
            send_block(sb_0, rr_f, n // 2, 2, r_f)
            keep_own(sb_0, rr_f, n // 2, r_f)

    def summed(way, rr, h, s):
        block = rr[h, :, s]
        return dot_tn(onehot[way, h, s], block.reshape(4 * SLOT, HALF))

    def return_far(way, rr, ag, hop, arriving):
        copies = []
        for h in (0, 1):
            arriving[h].wait()
            received(arriving[h, 2])
            s = at(h, 2)
            ag[h, s] = summed(way, rr, h, s).astype(bf16)
            for k, off in enumerate((1, 3)):
                cp = sems.remote(ag.at[h, s, pl.ds(64 * k, 64)], hop.at[h, k], peer(h, off))
                cp.start()
                copies.append(cp)
        return copies

    def return_near(way, rr, ag, hop, last, arriving, far):
        copies = []
        for h in (0, 1):
            for k, off in enumerate((1, 3)):
                received(arriving[h, off])
                s = at(h, off)
                part = summed(way, rr, h, s)
                far[2 * h + k].wait_recv()
                rows = slice(64 * k, 64 * k + 64)
                rest = slice(64 * (1 - k), 64 * (1 - k) + 64)
                ag[h, s, rest] = part[rest].astype(bf16)
                ag[h, s, rows] = (part[rows] + hop[h, k].astype(f32)).astype(bf16)
                cp = sems.remote(ag.at[h, s], last.at[h, k], peer(h, off))
                cp.start()
                copies.append(cp)
        return copies

    def return_own(way, rr, arriving):
        for h in (0, 1):
            received(arriving[h, 0])
            own[h] = summed(way, rr, h, spot[h])

    def total_of(last, near):
        for h in (0, 1):
            received(near[2 * h : 2 * h + 2])
            own[h] += last[h, 0].astype(f32) + last[h, 1].astype(f32)

    far_b = return_far(1, rr_b, ag_xb, hop_b, r_b)

    def grad_image(i):
        zi, xi = i // 2, 2 * (i % 2)
        for h in (0, 1):
            span = slice(h * HALF, (h + 1) * HALF)
            shift = jnp.zeros((1, HALF), f32)
            scale = jnp.zeros((1, HALF), f32)
            for par in (0, 1):
                cut = slice(par * CAP, (par + 1) * CAP)
                center, inv = [
                    jnp.concatenate([cols[0, i, cut, k], cols[1, i, cut, k]], axis=0)
                    for k in (MU_B, ISTD_B)
                ]
                grad = slots_of(sb_1, h, zi, xi + par)
                normed = (slots_of(sl_xb, h, zi, xi + par) - center) * inv
                shift += jnp.sum(grad, axis=0, keepdims=True)
                scale += jnp.sum(grad * normed, axis=0, keepdims=True)
            stat[0, pl.ds(i, 1), span] = shift
            stat[1, pl.ds(i, 1), span] = scale

    loop(IMAGES, grad_image)
    sum_z = [
        sems.remote(
            stat.at[:, :, pl.ds(pl.multiple_of(at(0, off) * TILE, TILE), TILE)],
            st_z.at[z],
            peer(0, off),
        )
        for off in (1, 2, 3)
    ]
    for cp in sum_z:
        cp.start()
    for h in (0, 1):
        for rel in (1, 3):
            send_block(sb_0, rr_f, h, rel, r_f)
    near_b = return_near(1, rr_b, ag_xb, hop_b, last_b, r_b, far_b)

    for cp in sum_z:
        cp.wait()
    st_z[z] = stat[:, :, pl.ds(pl.multiple_of(z * TILE, TILE), TILE)]
    st_2[...] = st_z[0] + st_z[1] + st_z[2] + st_z[3]
    sum_x = [
        sems.remote(
            st_2.at[:, :, pl.ds(pl.multiple_of(at(1, off) * TOK, TOK), TOK)],
            st_x.at[x],
            peer(1, off),
        )
        for off in (1, 2, 3)
    ]
    for cp in sum_x:
        cp.start()

    far_f = return_far(0, rr_f, ag_xf, hop_f, r_f)
    for h in (0, 1):
        send_block(sb_0, rr_f, h, 0, r_f)
    return_own(1, rr_b, r_b)
    for cp in sum_x:
        cp.wait()
    st_x[x] = st_2[:, :, pl.ds(pl.multiple_of(x * TOK, TOK), TOK)]
    own_part = fin.at[:, :, pl.ds(pl.multiple_of(me * TOK, TOK), TOK)]
    own_part[...] = st_x[0] + st_x[1] + st_x[2] + st_x[3]
    give_x = [sems.remote(own_part, own_part, peer(1, off)) for off in (1, 2, 3)]
    for cp in give_x:
        cp.start()

    near_f = return_near(0, rr_f, ag_xf, hop_f, last_f, r_f, far_f)
    total_of(last_b, near_b)
    for cp in give_x:
        cp.wait()
    own_part = fin.at[:, :, pl.ds(pl.multiple_of(z * TILE, TILE), TILE)]
    give_z = [sems.remote(own_part, own_part, peer(0, off)) for off in (1, 2, 3)]
    for cp in give_z:
        cp.start()
    own_scale = modulation_of(1, me // 2, 1)

    def input_grads(c):
        at_rows = pl.ds(pl.multiple_of(c * 32, 32), 32)
        parts = []
        for h in (0, 1):
            parts.append(ag_xb[h, spot[h], at_rows].astype(f32))
        total = jnp.sum(parts[0], axis=1, keepdims=True) + jnp.sum(parts[1], axis=1, keepdims=True)
        center = total * (1.0 / D)
        parts = [part - center for part in parts]
        total = jnp.sum(parts[0] * parts[0], axis=1, keepdims=True) + jnp.sum(
            parts[1] * parts[1], axis=1, keepdims=True
        )
        inv = lax.rsqrt(total * (1.0 / D) + epsilon)
        normed = [part * inv for part in parts]
        grads = []
        for h in (0, 1):
            span = slice(h * HALF, (h + 1) * HALF)
            grads.append(own[h, at_rows] * (1.0 + own_scale[:, span]))
        mean = (
            jnp.sum(grads[0], axis=1, keepdims=True) + jnp.sum(grads[1], axis=1, keepdims=True)
        ) * (1.0 / D)
        slope = (
            jnp.sum(grads[0] * normed[0], axis=1, keepdims=True)
            + jnp.sum(grads[1] * normed[1], axis=1, keepdims=True)
        ) * (1.0 / D)
        for h in (0, 1):
            span = slice(h * HALF, (h + 1) * HALF)
            dyv = ag_dy[h, spot[h], at_rows].astype(f32)
            part = dyv + inv * (grads[h] - mean - normed[h] * slope)
            res[at_rows, span] = part.astype(bf16)

    loop(4, input_grads)
    back_copy = sems.copy(res, out_b)
    back_copy.start()

    return_own(0, rr_f, r_f)
    total_of(last_f, near_f)
    back_copy.wait()
    own_gate = modulation_of(0, me // 2, 2)

    def outputs(c):
        at_rows = pl.ds(pl.multiple_of(c * 32, 32), 32)
        for h in (0, 1):
            span = slice(h * HALF, (h + 1) * HALF)
            part = ag_xf[h, spot[h], at_rows].astype(f32) + own_gate[:, span] * own[h, at_rows]
            res[at_rows, span] = part.astype(bf16)

    loop(4, outputs)
    front_copy = sems.copy(res, out_f)
    front_copy.start()
    for cp in give_z:
        cp.wait()
    fin_copy = sems.copy(fin, fin_out)
    fin_copy.start()
    for copies in (r_b, r_f):
        for h in (0, 1):
            for rel in range(4):
                sent(copies[h, rel])
    sent(far_b + near_b + far_f + near_f)
    for cp in kept_late:
        cp.wait()
    front_copy.wait()
    fin_copy.wait()


def layer(routes_f, routes_b, times_f, times_b, table, router, xf, xb, dy, up, down):
    any_spec = pl.BlockSpec(memory_space=pl.ANY)
    vmem = pl.BlockSpec(memory_space=pltpu.VMEM)
    smem = pl.BlockSpec(memory_space=pltpu.SMEM)
    shape = jax.ShapeDtypeStruct
    gather = pltpu.VMEM((2, 4, TOK, HALF), bf16)
    slots = pltpu.VMEM((2, 4, 4, SLOT, HALF), bf16)
    return pl.pallas_call(
        layer_kernel,
        out_shape=(
            shape((TOK, D), bf16),
            shape((TOK, D), bf16),
            shape((2, IMAGES, SLOT, D), bf16),
            shape((2, IMAGES, SLOT, D), bf16),
            shape((2, ROWS, FF), bf16),
            shape((2, ROWS, FF), bf16),
            shape((7, 8, D), f32),
        ),
        in_specs=[vmem, vmem, smem, smem, vmem, vmem] + [any_spec] * 5,
        out_specs=tuple([any_spec] * 7),
        scratch_shapes=[
            pltpu.SemaphoreType.DMA((N_REMOTE,)),
            pltpu.SemaphoreType.DMA((N_REMOTE,)),
            pltpu.SemaphoreType.DMA((N_LOCAL,)),
            pltpu.VMEM((4, 4, 8, TOK), f32),
            pltpu.VMEM((2, 2, 4, 4 * SLOT, TOK), bf16),
            gather,
            gather,
            gather,
            slots,
            slots,
            slots,
            slots,
            slots,
            slots,
            slots,
            pltpu.VMEM((2, 2, 64, HALF), bf16),
            pltpu.VMEM((2, 2, 64, HALF), bf16),
            pltpu.VMEM((2, 2, TOK, HALF), bf16),
            pltpu.VMEM((2, 2, TOK, HALF), bf16),
            pltpu.VMEM((2, TOK, HALF), f32),
            pltpu.VMEM((2, FF, D), bf16),
            pltpu.VMEM((2, FF, D), bf16),
            pltpu.VMEM((2, IMAGES, SLOT, D), bf16),
            pltpu.VMEM((2, IMAGES, SLOT, D), bf16),
            pltpu.VMEM((2, ROWS, FF), f32),
            pltpu.VMEM((2, ROWS, FF), bf16),
            pltpu.VMEM((2, ROWS, FF), bf16),
            pltpu.VMEM((2, IMAGES, SLOT, TILE), f32),
            pltpu.VMEM((3, 2 * IMAGES, D), f32),
            pltpu.VMEM((2, IMAGES, SLOT, 8), f32),
            pltpu.VMEM((2, 2, ROWS, EXPERTS), bf16),
            pltpu.VMEM((7, 8, D), f32),
            pltpu.VMEM((4, 7, 8, TILE), f32),
            pltpu.VMEM((7, 8, TILE), f32),
            pltpu.VMEM((4, 7, 8, TOK), f32),
            pltpu.VMEM((7, 8, D), f32),
            pltpu.VMEM((TOK, D), bf16),
        ],
        compiler_params=pltpu.CompilerParams(
            collective_id=0, has_side_effects=True, vmem_limit_bytes=63 << 20
        ),
        cost_estimate=pl.CostEstimate(
            flops=13_000_000_000, bytes_accessed=30_000_000, transcendentals=2_000_000
        ),
        name="moe_layer",
    )(routes_f, routes_b, times_f, times_b, table, router, xf, xb, dy, up, down)


def gradients_kernel(times, pg, hid, xm, og, sums, up_out, down_out, router_out, table_out, pg_t, hid_t):
    n = pl.program_id(1)

    @pl.when(n == 0)
    def _():
        pg_t[...] = pg[0].T
        hid_t[...] = hid[0].T

    up_out[0, 0] = dot(pg_t[...], xm[0]).astype(bf16)
    down_out[0, 0] = dot(hid_t[...], og[0]).astype(bf16)

    @pl.when((n == 0) & (pl.program_id(0) == 0))
    def _():
        for k in range(EXPERTS // 8):
            router_out[0, 8 * k : 8 * k + 8] = sums[3 + k]
        steps = lax.broadcasted_iota(jnp.int32, (16, 1), 0)
        for c in range(3):
            total = jnp.zeros((16, D), f32)
            for i in range(IMAGES):
                total += jnp.where(steps == times[0, i], sums[c, i : i + 1, :], 0.0)
            table_out[0, c] = total


def gradients(times, pg, hid, xm, og, sums):
    shape = jax.ShapeDtypeStruct
    whole = lambda j, n: (j, 0, 0)
    part = lambda j, n: (j, 0, n)
    return pl.pallas_call(
        gradients_kernel,
        grid=(2, 2),
        out_shape=(
            shape((1, 2, FF, D), bf16),
            shape((1, 2, FF, D), bf16),
            shape((1, EXPERTS, D), f32),
            shape((1, 3, 16, D), f32),
        ),
        in_specs=[
            pl.BlockSpec(memory_space=pltpu.SMEM),
            pl.BlockSpec((1, ROWS, FF), whole),
            pl.BlockSpec((1, ROWS, FF), whole),
            pl.BlockSpec((1, ROWS, HALF), part),
            pl.BlockSpec((1, ROWS, HALF), part),
            pl.BlockSpec((7, 8, D), lambda j, n: (0, 0, 0)),
        ],
        out_specs=(
            pl.BlockSpec((1, 1, FF, HALF), lambda j, n: (0, j, 0, n)),
            pl.BlockSpec((1, 1, FF, HALF), lambda j, n: (0, j, 0, n)),
            pl.BlockSpec((1, EXPERTS, D), lambda j, n: (0, 0, 0)),
            pl.BlockSpec((1, 3, 16, D), lambda j, n: (0, 0, 0, 0)),
        ),
        scratch_shapes=[pltpu.VMEM((FF, ROWS), bf16), pltpu.VMEM((FF, ROWS), bf16)],
        compiler_params=pltpu.CompilerParams(vmem_limit_bytes=60 << 20),
        cost_estimate=pl.CostEstimate(
            flops=4_500_000_000, bytes_accessed=22_000_000, transcendentals=0
        ),
        name="weight_grads",
    )(times, pg, hid, xm, og, sums)


def passed_along(value, steps):
    count = lax.axis_size("section")
    pairs = [(source, (source + steps) % count) for source in range(count)]
    return lax.ppermute(value, "section", pairs)


def per_device(
    forward_input,
    backward_input,
    backward_grad,
    forward_routes,
    backward_routes,
    forward_times,
    backward_times,
    modulation,
    router_weight,
    expert_up,
    expert_down,
):
    block_out, input_part, rows, out_grad, hidden, pre_grad, sums = layer(
        forward_routes[0].T,
        backward_routes[0].T,
        forward_times,
        backward_times,
        modulation.transpose(0, 2, 1, 3),
        router_weight.transpose(0, 2, 1),
        forward_input,
        backward_input,
        backward_grad,
        expert_up.transpose(0, 1, 3, 2),
        expert_down,
    )
    input_grad = passed_along(input_part, -1)
    forward_output = passed_along(block_out, 1)
    rows = rows.reshape(2, ROWS, D)
    out_grad = out_grad.reshape(2, ROWS, D)
    up_grad, down_grad, router_grad, table_grad = gradients(
        backward_times, pre_grad, hidden, rows, out_grad, sums
    )
    return (
        forward_output[None],
        input_grad[None],
        up_grad.transpose(0, 1, 3, 2),
        down_grad,
        router_grad.transpose(0, 2, 1),
        table_grad.transpose(0, 2, 1, 3),
    )


def solution(mesh):
    placed = (
        P("section", "ep", None),
        P("section", "ep", None),
        P("section", "ep", None),
        P("section", "ep", None),
        P("section", "ep", None),
        P("section", None),
        P("section", None),
        P("section", None, None, None),
        P("section", None, None),
        P("section", "ep", None, None),
        P("section", "ep", None, None),
    )
    return jax.shard_map(
        per_device,
        mesh=mesh,
        in_specs=placed,
        out_specs=(
            P("section", "ep", None),
            P("section", "ep", None),
            P("section", "ep", None, None),
            P("section", "ep", None, None),
            P("section", None, None),
            P("section", None, None, None),
        ),
        check_vma=False,
    )
```

```python
import jax
import jax.numpy as jnp
from jax import lax
from jax.experimental import pallas as pl
from jax.experimental.pallas import tpu as pltpu
from jax.sharding import PartitionSpec as P

D = 2048
HALF = 1024
FF = 704
TOK = 128
CAP = 24
SLOT = 2 * CAP
EXPERTS = 32
IMAGES = 8
ROWS = IMAGES * SLOT
STAT = 56
TILE = 512
epsilon = 1e-06
MESH = pl.DeviceIdType.MESH
f32 = jnp.float32
bf16 = jnp.bfloat16
FF_TILES = ((0, 256), (256, 512), (512, 704))
PROB, PROB2, OTHER, PGRAD, MU_B, ISTD_B = (slice(k, k + 1) for k in range(6))
GELU_A = 0.7978845608028654
GELU_B = 0.044715


def dot(a, b):
    return jnp.dot(a, b, preferred_element_type=f32)


def dot_nt(a, b):
    return lax.dot_general(a, b, (((1,), (1,)), ((), ())), preferred_element_type=f32)


def dot_tn(a, b):
    return lax.dot_general(a, b, (((0,), (0,)), ((), ())), preferred_element_type=f32)


def gelu(values):
    inner = jnp.tanh(GELU_A * (values + GELU_B * values * values * values))
    return 0.5 * values * (1.0 + inner)


def gelu_slope(values):
    square = values * values
    inner = jnp.tanh(GELU_A * (values + GELU_B * values * square))
    outer = 0.5 * values * (1.0 - inner * inner) * (GELU_A * (1.0 + 3.0 * GELU_B * square))
    return 0.5 * (1.0 + inner) + outer


def loop(count, body):
    def step(index, carry):
        body(index)
        return carry

    lax.fori_loop(0, count, step, 0)


class Sems:
    def __init__(self, send, recv, local):
        self.send, self.recv, self.local = send, recv, local
        self.remote_used = self.local_used = 0

    def remote(self, src, dst, device):
        k = self.remote_used
        self.remote_used += 1
        return pltpu.make_async_remote_copy(
            src_ref=src,
            dst_ref=dst,
            send_sem=self.send.at[k],
            recv_sem=self.recv.at[k],
            device_id=device,
            device_id_type=MESH,
        )

    def copy(self, src, dst):
        k = self.local_used
        self.local_used += 1
        return pltpu.make_async_copy(src, dst, self.local.at[k])


N_REMOTE = 200
N_LOCAL = 40


def layer_kernel(
    routes_f,
    routes_b,
    times_f,
    times_b,
    table_ref,
    router_ref,
    xf_hbm,
    xb_hbm,
    dy_hbm,
    up_hbm,
    down_hbm,
    out_f,
    out_b,
    xm_out,
    og_out,
    hid_out,
    pg_out,
    fin_out,
    send_sem,
    recv_sem,
    local_sem,
    meta,
    onehot,
    ag_xb,
    ag_dy,
    ag_xf,
    sb_0,
    sb_1,
    sl_xb,
    sl_dy,
    sl_xf,
    rr_b,
    rr_f,
    hop_b,
    hop_f,
    last_b,
    last_f,
    own,
    up,
    down,
    xm,
    og,
    pre,
    hid,
    pgr,
    tile_out,
    modr,
    cols,
    wrow,
    stat,
    st_z,
    st_2,
    st_x,
    fin,
    res,
):
    section = lax.axis_index("section")
    me = lax.axis_index("ep")
    z, x = me // 4, me % 4
    sems = Sems(send_sem, recv_sem, local_sem)

    def peer(axis, off):
        if axis == 0:
            return (section, lax.rem(z + off + 4, 4) * 4 + x)
        return (section, z * 4 + lax.rem(x + off + 4, 4))

    spot = (z, x)

    def at(axis, off):
        return lax.rem(spot[axis] + off + 4, 4)

    barrier = pltpu.get_barrier_semaphore()
    for axis in (0, 1):
        for off in (1, 2, 3):
            pl.semaphore_signal(barrier, inc=1, device_id=peer(axis, off), device_id_type=MESH)

    own_copies = []
    for source, ag in ((xb_hbm, ag_xb), (dy_hbm, ag_dy), (xf_hbm, ag_xf)):
        for h in (0, 1):
            cp = sems.copy(source.at[0, :, pl.ds(h * HALF, HALF)], ag.at[h, spot[h]])
            cp.start()
            own_copies.append(cp)
    up_copy = sems.copy(up_hbm.at[0], up)
    down_copy = sems.copy(down_hbm.at[0], down)

    expert_rows = lax.broadcasted_iota(jnp.int32, (EXPERTS, TOK), 0).astype(f32)
    earlier = (
        lax.broadcasted_iota(jnp.int32, (TOK, TOK), 0)
        < lax.broadcasted_iota(jnp.int32, (TOK, TOK), 1)
    ).astype(bf16)
    for way in (0, 1):
        routes = routes_b if way else routes_f
        e0 = routes[0:1, :].astype(f32)
        e1 = routes[1:2, :].astype(f32)
        o0 = (expert_rows == e0).astype(f32)
        o1 = (expert_rows == e1).astype(f32)
        rank = dot((o0 + o1).astype(bf16), earlier)
        s0 = e0 * CAP + jnp.sum(o0 * rank, axis=0, keepdims=True)
        s1 = e1 * CAP + jnp.sum(o1 * rank, axis=0, keepdims=True)
        for k, row in enumerate((s0, s1, e0, e1)):
            meta[x, z, 4 * way + k : 4 * way + k + 1, :] = row

    pl.semaphore_wait(barrier, 6)

    meta_z = [sems.remote(meta.at[x, z], meta.at[x, z], peer(0, off)) for off in (1, 2, 3)]
    for cp in meta_z:
        cp.start()

    def gather_start(ag, source):
        copies = []
        for off in (1, 3):
            for h in (0, 1):
                rows = source.at[0, :, pl.ds(h * HALF, HALF)]
                cp = sems.remote(rows, ag.at[h, spot[h]], peer(h, off))
                cp.start()
                copies.append(cp)
        return copies

    def gather_forward(ag, first):
        copies = []
        for k, off in enumerate((1, 3)):
            for h in (0, 1):
                first[2 * k + h].wait_recv()
                block = ag.at[h, at(h, -off), pl.ds(64 * k, 64)]
                cp = sems.remote(block, block, peer(h, off))
                cp.start()
                copies.append(cp)
        return copies

    g_xb = gather_start(ag_xb, xb_hbm)

    time_rows = lax.broadcasted_iota(jnp.int32, (2 * IMAGES, 16), 0)
    time_of = jnp.zeros((2 * IMAGES, 16), jnp.int32)
    for i in range(IMAGES):
        time_of = jnp.where(time_rows == i, times_f[0, i], time_of)
        time_of = jnp.where(time_rows == IMAGES + i, times_b[0, i], time_of)
    chosen = (time_of == lax.broadcasted_iota(jnp.int32, (2 * IMAGES, 16), 1)).astype(f32)
    for c in range(3):
        modr[c] = dot(chosen.astype(bf16), table_ref[0, c])

    def modulation_of(way, i, c, span=slice(0, D)):
        return modr[c, pl.ds(i + IMAGES * way, 1), span]

    for cp in meta_z:
        cp.wait()
    meta_x = [sems.remote(meta.at[x], meta.at[x], peer(1, off)) for off in (1, 2, 3)]
    for cp in meta_x:
        cp.start()
    g_dy = gather_start(ag_dy, dy_hbm)
    for cp in own_copies:
        cp.wait()

    slot_rows = lax.broadcasted_iota(jnp.int32, (4 * SLOT, TOK), 0)

    def build_onehot(way, h):
        if h == 0:
            ids = slot_rows + z * 192
        else:
            block = (
                (slot_rows >= 48).astype(jnp.int32)
                + (slot_rows >= 96).astype(jnp.int32)
                + (slot_rows >= 144).astype(jnp.int32)
            )
            ids = slot_rows + block * 144 + x * SLOT
        ids = ids.astype(f32)

        def one(s):
            block = meta[x, s] if h == 0 else meta[s, z]
            s0 = block[4 * way : 4 * way + 1, :]
            s1 = block[4 * way + 1 : 4 * way + 2, :]
            onehot[way, h, s] = ((ids == s0).astype(f32) + (ids == s1).astype(f32)).astype(bf16)

        loop(4, one)

    def pack(way, ag, sb, h, s):
        for n in (0, 1):
            part = dot(onehot[way, h, s], ag[h, s, :, n * TILE : (n + 1) * TILE])
            sb[h, :, s, :, n * TILE : (n + 1) * TILE] = part.astype(bf16).reshape(4, SLOT, TILE)

    def send_block(sb, rb, h, rel, copies):
        axis, s = 1 - h, at(h, rel)
        copies[h, rel] = []
        for off in (2, 1, 3):
            cp = sems.remote(
                sb.at[h, at(axis, off), s], rb.at[h, spot[axis], s], peer(axis, off)
            )
            cp.start()
            copies[h, rel].append(cp)

    def keep_own(sb, rb, h, copies):
        axis = 1 - h
        cp = sems.copy(sb.at[h, spot[axis]], rb.at[h, spot[axis]])
        cp.start()
        copies[h] = cp

    def pack_send(way, ag, sb, rb, rel, copies):
        for h in (0, 1):
            pack(way, ag, sb, h, at(h, rel))
            send_block(sb, rb, h, rel, copies)

    def all_sent(copies):
        for h in (0, 1):
            copies[h].wait()
            for rel in range(4):
                for cp in copies[h, rel]:
                    cp.wait_send()

    def all_arrived(copies):
        for h in (0, 1):
            for rel in range(4):
                for cp in copies[h, rel]:
                    cp.wait_recv()

    def received(copies):
        for cp in copies:
            cp.wait_recv()

    def sent(copies):
        for cp in copies:
            cp.wait_send()

    d_xb, d_dy, d_xf = {}, {}, {}
    build_onehot(1, 0)
    f_xb = gather_forward(ag_xb, g_xb)
    for h in (0, 1):
        if h:
            for cp in meta_x:
                cp.wait()
            build_onehot(1, 1)
        for rel in (0, 1, 3):
            pack(1, ag_xb, sb_0, h, at(h, rel))
            send_block(sb_0, sl_xb, h, rel, d_xb)
    f_dy = gather_forward(ag_dy, g_dy)
    received(f_xb)
    pack_send(1, ag_xb, sb_0, sl_xb, 2, d_xb)
    for rel in (0, 1, 3):
        pack_send(1, ag_dy, sb_1, sl_dy, rel, d_dy)
    g_xf = gather_start(ag_xf, xf_hbm)
    received(f_dy)
    pack_send(1, ag_dy, sb_1, sl_dy, 2, d_dy)
    up_copy.start()
    down_copy.start()
    for h in (0, 1):
        keep_own(sb_0, sl_xb, h, d_xb)
        keep_own(sb_1, sl_dy, h, d_dy)
    build_onehot(0, 0)
    build_onehot(0, 1)

    def slots_of(sl, h, zi, xi):
        block = sl[h, xi, zi] if h == 0 else sl[h, zi, xi]
        return block.astype(f32)

    def by_expert(sl, h, i, j):
        zi, xi = i // 2, 2 * (i % 2)
        first = slots_of(sl, h, zi, xi)[j * CAP : (j + 1) * CAP]
        second = slots_of(sl, h, zi, xi + 1)[j * CAP : (j + 1) * CAP]
        return jnp.concatenate([first, second], axis=0)

    cap_rows = lax.broadcasted_iota(jnp.int32, (CAP, TOK), 0)

    def normalize(sl, way):
        def one(i):
            zi, xi = i // 2, 2 * (i % 2)
            shift, scale = modulation_of(way, i, 0), modulation_of(way, i, 1)
            for j in (0, 1):
                left, right = by_expert(sl, 0, i, j), by_expert(sl, 1, i, j)
                total = jnp.sum(left, axis=1, keepdims=True) + jnp.sum(right, axis=1, keepdims=True)
                center = total * (1.0 / D)
                left, right = left - center, right - center
                total = jnp.sum(left * left, axis=1, keepdims=True) + jnp.sum(
                    right * right, axis=1, keepdims=True
                )
                inv = lax.rsqrt(total * (1.0 / D) + epsilon)
                for h, part in ((0, left), (1, right)):
                    span = slice(h * HALF, (h + 1) * HALF)
                    mixed = part * inv * (1.0 + scale[:, span]) + shift[:, span]
                    xm[j, i, :, span] = mixed.astype(bf16)
                if way:
                    cols[j, i, :, MU_B] = center
                    cols[j, i, :, ISTD_B] = inv
                ids = (cap_rows + (me * SLOT + j * CAP)).astype(f32)
                found = []
                for par in (0, 1):
                    block = meta[xi + par, zi]
                    s0, s1, e0, e1 = [
                        block[4 * way + k : 4 * way + k + 1, :] for k in range(4)
                    ]
                    hit = jnp.where(ids == s0, e1, 0.0) + jnp.where(ids == s1, e0, 0.0)
                    found.append(jnp.sum(hit, axis=1, keepdims=True))
                cols[j, i, :, OTHER] = jnp.concatenate(found, axis=0)

        loop(IMAGES, one)

    lane = lax.broadcasted_iota(jnp.int32, (ROWS, EXPERTS), 1)

    def picks(j):
        own = (lane == 2 * me + j).astype(f32)
        return own - (lane.astype(f32) == cols[j, :, :, OTHER].reshape(ROWS, 1)).astype(f32)

    def experts_up(keep):
        def one(j):
            rows = xm[j].reshape(ROWS, D)
            logits = dot_nt(rows, router_ref[0])
            gap = jnp.sum(logits * picks(j), axis=1, keepdims=True)
            chance = 1.0 / (1.0 + jnp.exp(-gap))
            cols[j, :, :, PROB] = chance.reshape(IMAGES, SLOT, 1)
            if keep:
                cols[j, :, :, PROB2] = (chance * (1.0 / (1.0 + jnp.exp(gap)))).reshape(IMAGES, SLOT, 1)
            for f0, f1 in FF_TILES:
                part = dot_nt(rows, up[j, f0:f1, :])
                if keep:
                    pre[j, :, f0:f1] = part
                hid[j, :, f0:f1] = gelu(part).astype(bf16)

        loop(2, one)

    def put_rows(sb, h, n):
        def one(i):
            zi, xi = i // 2, 2 * (i % 2)
            a, b = tile_out[0, i], tile_out[1, i]
            for par in (0, 1):
                block = jnp.concatenate(
                    [a[par * CAP : (par + 1) * CAP], b[par * CAP : (par + 1) * CAP]], axis=0
                ).astype(bf16)
                span = slice(n * TILE, (n + 1) * TILE)
                if h == 0:
                    sb[h, xi + par, zi, :, span] = block
                else:
                    sb[h, zi, xi + par, :, span] = block

        loop(IMAGES, one)

    all_arrived(d_xb)
    all_sent(d_xb)
    sent(g_xb + f_xb)
    normalize(sl_xb, 1)
    f_xf = gather_forward(ag_xf, g_xf)
    up_copy.wait()
    experts_up(True)
    kept = [sems.copy(xm, xm_out), sems.copy(hid, hid_out)]
    for cp in kept:
        cp.start()
    down_copy.wait()

    for n in range(D // TILE):
        span = slice(n * TILE, (n + 1) * TILE)

        def out_tile(j):
            part = dot(hid[j], down[j, :, span]).astype(bf16)
            og[j, :, :, span] = part.reshape(IMAGES, SLOT, TILE)

        loop(2, out_tile)

    for h in (0, 1):
        for rel in (0, 1, 3):
            pack(0, ag_xf, sb_0, h, at(h, rel))
    for rel in (0, 1, 3):
        for h in (0, 1):
            sent(d_dy[h, rel])
    for rel in (0, 1, 3):
        for h in (0, 1):
            send_block(sb_0, sl_xf, h, rel, d_xf)
    received(f_xf)
    pack_send(0, ag_xf, sb_0, sl_xf, 2, d_xf)
    for h in (0, 1):
        keep_own(sb_0, sl_xf, h, d_xf)
    all_arrived(d_dy)
    for h in (0, 1):
        d_dy[h].wait()
        sent(d_dy[h, 2])
    sent(g_dy + f_dy)

    cols[:, :, :, PGRAD] = jnp.zeros((2, IMAGES, SLOT, 1), f32)

    def out_image(i):
        for h in (0, 1):
            span = slice(h * HALF, (h + 1) * HALF)
            gate = modulation_of(1, i, 2, span)
            total = jnp.zeros((1, HALF), f32)
            for j in (0, 1):
                out = og[j, i, :, span].astype(f32)
                dyv = by_expert(sl_dy, h, i, j)
                chance = cols[j, i, :, PROB]
                mix = (dyv * gate).astype(bf16).astype(f32)
                cols[j, i, :, PGRAD] += jnp.sum(out * mix, axis=1, keepdims=True)
                total += jnp.sum(out * dyv * chance, axis=0, keepdims=True)
                og[j, i, :, span] = (chance.astype(bf16).astype(f32) * mix).astype(bf16)
            stat[2, pl.ds(i, 1), span] = total

    loop(IMAGES, out_image)

    def hidden_grad(j):
        rows = og[j].reshape(ROWS, D)
        for f0, f1 in FF_TILES:
            part = dot_nt(rows, down[j, f0:f1, :])
            pgr[j, :, f0:f1] = (part * gelu_slope(pre[j, :, f0:f1])).astype(bf16)
        weight = picks(j) * (cols[j, :, :, PGRAD] * cols[j, :, :, PROB2]).reshape(ROWS, 1)
        high = weight.astype(bf16)
        wrow[j, 0] = high
        wrow[j, 1] = (weight - high.astype(f32)).astype(bf16)

    loop(2, hidden_grad)
    r_b, r_f = {}, {}
    for n in range(D // TILE):
        span = slice(n * TILE, (n + 1) * TILE)

        def grad_tile(j):
            part = dot(pgr[j], up[j, :, span]).astype(bf16).astype(f32)
            rows = router_ref[0, :, span]
            part += dot(wrow[j, 0], rows) + dot(wrow[j, 1], rows)
            tile_out[j] = part.reshape(IMAGES, SLOT, TILE)

        loop(2, grad_tile)
        put_rows(sb_1, n // 2, n % 2)
        if n % 2:
            for rel in (2, 1, 3, 0):
                send_block(sb_1, rr_b, n // 2, rel, r_b)
            keep_own(sb_1, rr_b, n // 2, r_b)

    kept_late = [sems.copy(og, og_out), sems.copy(pgr, pg_out)]
    for cp in kept_late:
        cp.start()

    for n in range(D // TILE):
        span = slice(n * TILE, (n + 1) * TILE)
        rg = jnp.zeros((EXPERTS, TILE), f32)
        for j in (0, 1):
            block = xm[j, :, :, span].reshape(ROWS, TILE)
            rg += dot_tn(wrow[j, 0], block) + dot_tn(wrow[j, 1], block)
        for k in range(EXPERTS // 8):
            stat[3 + k, :, span] = rg[8 * k : 8 * k + 8]

    def grad_image(i):
        zi, xi = i // 2, 2 * (i % 2)
        for h in (0, 1):
            span = slice(h * HALF, (h + 1) * HALF)
            shift = jnp.zeros((1, HALF), f32)
            scale = jnp.zeros((1, HALF), f32)
            for par in (0, 1):
                cut = slice(par * CAP, (par + 1) * CAP)
                center, inv = [
                    jnp.concatenate([cols[0, i, cut, k], cols[1, i, cut, k]], axis=0)
                    for k in (MU_B, ISTD_B)
                ]
                grad = slots_of(sb_1, h, zi, xi + par)
                normed = (slots_of(sl_xb, h, zi, xi + par) - center) * inv
                shift += jnp.sum(grad, axis=0, keepdims=True)
                scale += jnp.sum(grad * normed, axis=0, keepdims=True)
            stat[0, pl.ds(i, 1), span] = shift
            stat[1, pl.ds(i, 1), span] = scale

    loop(IMAGES, grad_image)
    sum_z = [
        sems.remote(
            stat.at[:, :, pl.ds(pl.multiple_of(at(0, off) * TILE, TILE), TILE)],
            st_z.at[z],
            peer(0, off),
        )
        for off in (1, 2, 3)
    ]
    for cp in sum_z:
        cp.start()
    all_arrived(d_xf)
    all_sent(d_xf)
    sent(g_xf + f_xf)
    for cp in kept:
        cp.wait()
    normalize(sl_xf, 0)
    experts_up(False)
    for n in range(D // TILE):
        span = slice(n * TILE, (n + 1) * TILE)

        def give_tile(j):
            part = dot(hid[j], down[j, :, span]) * cols[j, :, :, PROB].reshape(ROWS, 1)
            tile_out[j] = part.reshape(IMAGES, SLOT, TILE)

        loop(2, give_tile)
        put_rows(sb_0, n // 2, n % 2)
        if n % 2:
            send_block(sb_0, rr_f, n // 2, 2, r_f)
            keep_own(sb_0, rr_f, n // 2, r_f)

    def summed(way, rr, h, s):
        block = rr[h, :, s]
        return dot_tn(onehot[way, h, s], block.reshape(4 * SLOT, HALF))

    def return_far(way, rr, ag, hop, arriving):
        copies = []
        for h in (0, 1):
            arriving[h].wait()
            received(arriving[h, 2])
            s = at(h, 2)
            ag[h, s] = summed(way, rr, h, s).astype(bf16)
            for k, off in enumerate((1, 3)):
                cp = sems.remote(ag.at[h, s, pl.ds(64 * k, 64)], hop.at[h, k], peer(h, off))
                cp.start()
                copies.append(cp)
        return copies

    def return_near(way, rr, ag, hop, last, arriving, far):
        copies = []
        for h in (0, 1):
            for k, off in enumerate((1, 3)):
                received(arriving[h, off])
                s = at(h, off)
                ag[h, s] = summed(way, rr, h, s).astype(bf16)
                rest = pl.ds(64 * (1 - k), 64)
                cp = sems.remote(ag.at[h, s, rest], last.at[h, k, rest], peer(h, off))
                cp.start()
                copies.append(cp)
        for h in (0, 1):
            for k, off in enumerate((1, 3)):
                s = at(h, off)
                far[2 * h + k].wait_recv()
                rows = pl.ds(64 * k, 64)
                ag[h, s, rows] = (ag[h, s, rows].astype(f32) + hop[h, k].astype(f32)).astype(bf16)
                cp = sems.remote(ag.at[h, s, rows], last.at[h, k, rows], peer(h, off))
                cp.start()
                copies.append(cp)
        return copies

    def return_own(way, rr, arriving):
        for h in (0, 1):
            received(arriving[h, 0])
            own[h] = summed(way, rr, h, spot[h])

    def total_of(last, near):
        received(near)
        for h in (0, 1):
            own[h] += last[h, 0].astype(f32) + last[h, 1].astype(f32)

    far_b = return_far(1, rr_b, ag_xb, hop_b, r_b)

    for cp in sum_z:
        cp.wait()
    st_z[z] = stat[:, :, pl.ds(pl.multiple_of(z * TILE, TILE), TILE)]
    st_2[...] = st_z[0] + st_z[1] + st_z[2] + st_z[3]
    sum_x = [
        sems.remote(
            st_2.at[:, :, pl.ds(pl.multiple_of(at(1, off) * TOK, TOK), TOK)],
            st_x.at[x],
            peer(1, off),
        )
        for off in (1, 2, 3)
    ]
    for cp in sum_x:
        cp.start()

    for h in (0, 1):
        for rel in (1, 3):
            send_block(sb_0, rr_f, h, rel, r_f)
    near_b = return_near(1, rr_b, ag_xb, hop_b, last_b, r_b, far_b)

    for cp in sum_x:
        cp.wait()
    st_x[x] = st_2[:, :, pl.ds(pl.multiple_of(x * TOK, TOK), TOK)]
    own_part = fin.at[:, :, pl.ds(pl.multiple_of(me * TOK, TOK), TOK)]
    own_part[...] = st_x[0] + st_x[1] + st_x[2] + st_x[3]
    give_x = [sems.remote(own_part, own_part, peer(1, off)) for off in (1, 2, 3)]
    for cp in give_x:
        cp.start()

    far_f = return_far(0, rr_f, ag_xf, hop_f, r_f)
    for h in (0, 1):
        send_block(sb_0, rr_f, h, 0, r_f)
    return_own(1, rr_b, r_b)
    for cp in give_x:
        cp.wait()
    own_part = fin.at[:, :, pl.ds(pl.multiple_of(z * TILE, TILE), TILE)]
    give_z = [sems.remote(own_part, own_part, peer(0, off)) for off in (1, 2, 3)]
    for cp in give_z:
        cp.start()
    near_f = return_near(0, rr_f, ag_xf, hop_f, last_f, r_f, far_f)
    total_of(last_b, near_b)
    own_scale = modulation_of(1, me // 2, 1)

    def input_grads(c):
        at_rows = pl.ds(pl.multiple_of(c * 32, 32), 32)
        parts = []
        for h in (0, 1):
            parts.append(ag_xb[h, spot[h], at_rows].astype(f32))
        total = jnp.sum(parts[0], axis=1, keepdims=True) + jnp.sum(parts[1], axis=1, keepdims=True)
        center = total * (1.0 / D)
        parts = [part - center for part in parts]
        total = jnp.sum(parts[0] * parts[0], axis=1, keepdims=True) + jnp.sum(
            parts[1] * parts[1], axis=1, keepdims=True
        )
        inv = lax.rsqrt(total * (1.0 / D) + epsilon)
        normed = [part * inv for part in parts]
        grads = []
        for h in (0, 1):
            span = slice(h * HALF, (h + 1) * HALF)
            grads.append(own[h, at_rows] * (1.0 + own_scale[:, span]))
        mean = (
            jnp.sum(grads[0], axis=1, keepdims=True) + jnp.sum(grads[1], axis=1, keepdims=True)
        ) * (1.0 / D)
        slope = (
            jnp.sum(grads[0] * normed[0], axis=1, keepdims=True)
            + jnp.sum(grads[1] * normed[1], axis=1, keepdims=True)
        ) * (1.0 / D)
        for h in (0, 1):
            span = slice(h * HALF, (h + 1) * HALF)
            dyv = ag_dy[h, spot[h], at_rows].astype(f32)
            part = dyv + inv * (grads[h] - mean - normed[h] * slope)
            res[at_rows, span] = part.astype(bf16)

    loop(4, input_grads)
    back_copy = sems.copy(res, out_b)
    back_copy.start()

    return_own(0, rr_f, r_f)
    total_of(last_f, near_f)
    back_copy.wait()
    own_gate = modulation_of(0, me // 2, 2)

    def outputs(c):
        at_rows = pl.ds(pl.multiple_of(c * 32, 32), 32)
        for h in (0, 1):
            span = slice(h * HALF, (h + 1) * HALF)
            part = ag_xf[h, spot[h], at_rows].astype(f32) + own_gate[:, span] * own[h, at_rows]
            res[at_rows, span] = part.astype(bf16)

    loop(4, outputs)
    front_copy = sems.copy(res, out_f)
    front_copy.start()
    for cp in give_z:
        cp.wait()
    fin_copy = sems.copy(fin, fin_out)
    fin_copy.start()
    for copies in (r_b, r_f):
        for h in (0, 1):
            for rel in range(4):
                sent(copies[h, rel])
    sent(far_b + near_b + far_f + near_f)
    for cp in kept_late:
        cp.wait()
    front_copy.wait()
    fin_copy.wait()


def layer(routes_f, routes_b, times_f, times_b, table, router, xf, xb, dy, up, down):
    any_spec = pl.BlockSpec(memory_space=pl.ANY)
    vmem = pl.BlockSpec(memory_space=pltpu.VMEM)
    smem = pl.BlockSpec(memory_space=pltpu.SMEM)
    shape = jax.ShapeDtypeStruct
    gather = pltpu.VMEM((2, 4, TOK, HALF), bf16)
    slots = pltpu.VMEM((2, 4, 4, SLOT, HALF), bf16)
    return pl.pallas_call(
        layer_kernel,
        out_shape=(
            shape((TOK, D), bf16),
            shape((TOK, D), bf16),
            shape((2, IMAGES, SLOT, D), bf16),
            shape((2, IMAGES, SLOT, D), bf16),
            shape((2, ROWS, FF), bf16),
            shape((2, ROWS, FF), bf16),
            shape((7, 8, D), f32),
        ),
        in_specs=[vmem, vmem, smem, smem, vmem, vmem] + [any_spec] * 5,
        out_specs=tuple([any_spec] * 7),
        scratch_shapes=[
            pltpu.SemaphoreType.DMA((N_REMOTE,)),
            pltpu.SemaphoreType.DMA((N_REMOTE,)),
            pltpu.SemaphoreType.DMA((N_LOCAL,)),
            pltpu.VMEM((4, 4, 8, TOK), f32),
            pltpu.VMEM((2, 2, 4, 4 * SLOT, TOK), bf16),
            gather,
            gather,
            gather,
            slots,
            slots,
            slots,
            slots,
            slots,
            slots,
            slots,
            pltpu.VMEM((2, 2, 64, HALF), bf16),
            pltpu.VMEM((2, 2, 64, HALF), bf16),
            pltpu.VMEM((2, 2, TOK, HALF), bf16),
            pltpu.VMEM((2, 2, TOK, HALF), bf16),
            pltpu.VMEM((2, TOK, HALF), f32),
            pltpu.VMEM((2, FF, D), bf16),
            pltpu.VMEM((2, FF, D), bf16),
            pltpu.VMEM((2, IMAGES, SLOT, D), bf16),
            pltpu.VMEM((2, IMAGES, SLOT, D), bf16),
            pltpu.VMEM((2, ROWS, FF), f32),
            pltpu.VMEM((2, ROWS, FF), bf16),
            pltpu.VMEM((2, ROWS, FF), bf16),
            pltpu.VMEM((2, IMAGES, SLOT, TILE), f32),
            pltpu.VMEM((3, 2 * IMAGES, D), f32),
            pltpu.VMEM((2, IMAGES, SLOT, 8), f32),
            pltpu.VMEM((2, 2, ROWS, EXPERTS), bf16),
            pltpu.VMEM((7, 8, D), f32),
            pltpu.VMEM((4, 7, 8, TILE), f32),
            pltpu.VMEM((7, 8, TILE), f32),
            pltpu.VMEM((4, 7, 8, TOK), f32),
            pltpu.VMEM((7, 8, D), f32),
            pltpu.VMEM((TOK, D), bf16),
        ],
        compiler_params=pltpu.CompilerParams(
            collective_id=0, has_side_effects=True, vmem_limit_bytes=63 << 20
        ),
        cost_estimate=pl.CostEstimate(
            flops=13_000_000_000, bytes_accessed=30_000_000, transcendentals=2_000_000
        ),
        name="moe_layer",
    )(routes_f, routes_b, times_f, times_b, table, router, xf, xb, dy, up, down)


def gradients_kernel(times, pg, hid, xm, og, sums, up_out, down_out, router_out, table_out, pg_t, hid_t):
    n = pl.program_id(1)

    @pl.when(n == 0)
    def _():
        pg_t[...] = pg[0].T
        hid_t[...] = hid[0].T

    up_out[0, 0] = dot(pg_t[...], xm[0]).astype(bf16)
    down_out[0, 0] = dot(hid_t[...], og[0]).astype(bf16)

    @pl.when((n == 0) & (pl.program_id(0) == 0))
    def _():
        for k in range(EXPERTS // 8):
            router_out[0, 8 * k : 8 * k + 8] = sums[3 + k]
        steps = lax.broadcasted_iota(jnp.int32, (16, 1), 0)
        for c in range(3):
            total = jnp.zeros((16, D), f32)
            for i in range(IMAGES):
                total += jnp.where(steps == times[0, i], sums[c, i : i + 1, :], 0.0)
            table_out[0, c] = total


def gradients(times, pg, hid, xm, og, sums):
    shape = jax.ShapeDtypeStruct
    whole = lambda j, n: (j, 0, 0)
    part = lambda j, n: (j, 0, n)
    return pl.pallas_call(
        gradients_kernel,
        grid=(2, 2),
        out_shape=(
            shape((1, 2, FF, D), bf16),
            shape((1, 2, FF, D), bf16),
            shape((1, EXPERTS, D), f32),
            shape((1, 3, 16, D), f32),
        ),
        in_specs=[
            pl.BlockSpec(memory_space=pltpu.SMEM),
            pl.BlockSpec((1, ROWS, FF), whole),
            pl.BlockSpec((1, ROWS, FF), whole),
            pl.BlockSpec((1, ROWS, HALF), part),
            pl.BlockSpec((1, ROWS, HALF), part),
            pl.BlockSpec((7, 8, D), lambda j, n: (0, 0, 0)),
        ],
        out_specs=(
            pl.BlockSpec((1, 1, FF, HALF), lambda j, n: (0, j, 0, n)),
            pl.BlockSpec((1, 1, FF, HALF), lambda j, n: (0, j, 0, n)),
            pl.BlockSpec((1, EXPERTS, D), lambda j, n: (0, 0, 0)),
            pl.BlockSpec((1, 3, 16, D), lambda j, n: (0, 0, 0, 0)),
        ),
        scratch_shapes=[pltpu.VMEM((FF, ROWS), bf16), pltpu.VMEM((FF, ROWS), bf16)],
        compiler_params=pltpu.CompilerParams(vmem_limit_bytes=60 << 20),
        cost_estimate=pl.CostEstimate(
            flops=4_500_000_000, bytes_accessed=22_000_000, transcendentals=0
        ),
        name="weight_grads",
    )(times, pg, hid, xm, og, sums)


def passed_along(value, steps):
    count = lax.axis_size("section")
    pairs = [(source, (source + steps) % count) for source in range(count)]
    return lax.ppermute(value, "section", pairs)


def per_device(
    forward_input,
    backward_input,
    backward_grad,
    forward_routes,
    backward_routes,
    forward_times,
    backward_times,
    modulation,
    router_weight,
    expert_up,
    expert_down,
):
    block_out, input_part, rows, out_grad, hidden, pre_grad, sums = layer(
        forward_routes[0].T,
        backward_routes[0].T,
        forward_times,
        backward_times,
        modulation.transpose(0, 2, 1, 3),
        router_weight.transpose(0, 2, 1),
        forward_input,
        backward_input,
        backward_grad,
        expert_up.transpose(0, 1, 3, 2),
        expert_down,
    )
    input_grad = passed_along(input_part, -1)
    forward_output = passed_along(block_out, 1)
    rows = rows.reshape(2, ROWS, D)
    out_grad = out_grad.reshape(2, ROWS, D)
    up_grad, down_grad, router_grad, table_grad = gradients(
        backward_times, pre_grad, hidden, rows, out_grad, sums
    )
    return (
        forward_output[None],
        input_grad[None],
        up_grad.transpose(0, 1, 3, 2),
        down_grad,
        router_grad.transpose(0, 2, 1),
        table_grad.transpose(0, 2, 1, 3),
    )


def solution(mesh):
    placed = (
        P("section", "ep", None),
        P("section", "ep", None),
        P("section", "ep", None),
        P("section", "ep", None),
        P("section", "ep", None),
        P("section", None),
        P("section", None),
        P("section", None, None, None),
        P("section", None, None),
        P("section", "ep", None, None),
        P("section", "ep", None, None),
    )
    return jax.shard_map(
        per_device,
        mesh=mesh,
        in_specs=placed,
        out_specs=(
            P("section", "ep", None),
            P("section", "ep", None),
            P("section", "ep", None, None),
            P("section", "ep", None, None),
            P("section", None, None),
            P("section", None, None, None),
        ),
        check_vma=False,
    )
```
